32 devices in a mesh: groups: 2 (over y), expert: 8 (over z, x), dp: 2 (over core).
Axes of the slice: x: 2, y: 2, z: 4, core: 2. Of those that a mesh axis runs over, the one named last changes fastest.
Arguments:
- tokens: bfloat16 [4096, 2048], P(('groups', 'expert', 'dp')), parts along dimension 0, may hold values from -6 to 6
- out_grad: bfloat16 [4096, 2048], P(('groups', 'expert', 'dp')), parts along dimension 0, may hold values from -6 to 6
- choices: int32 [4096, 8], P(('groups', 'expert', 'dp')), parts along dimension 0, may hold values from 0 to 127, as said below
- gates: bfloat16 [4096, 8], P(('groups', 'expert', 'dp')), parts along dimension 0, may hold values from 0.049804688 to 1
- gate_weight: bfloat16 [8, 2048, 192], P('expert'), may hold values from -0.125 to 0.125
- up_weight: bfloat16 [8, 2048, 192], P('expert'), may hold values from -0.125 to 0.125
- down_weight: bfloat16 [8, 192, 2048], P('expert'), may hold values from -0.21875 to 0.21875
Outputs:
- in_grad: bfloat16 [4096, 2048], P(('groups', 'expert', 'dp')), parts along dimension 0
- combine_grad: float32 [4096, 8], P(('groups', 'expert', 'dp')), parts along dimension 0
- gate_weight_grad: bfloat16 [16, 2048, 192], P(('groups', 'expert'), 'dp'), parts along dimension 0
- up_weight_grad: bfloat16 [16, 2048, 192], P(('groups', 'expert'), 'dp'), parts along dimension 0
- down_weight_grad: bfloat16 [16, 192, 2048], P(('groups', 'expert'), None, 'dp'), parts along dimension 0
The draws below stay inside these ranges and needn't reach their ends.
There are 2 independent parts, one for each index of `groups`. The reference program is written for one: setup_inputs(seed, part) draws one part's arguments, and reference() takes and returns one part's arrays. A program takes and returns all parts, laid end to end along the dimension named above; an argument that names none is the same for every part. Nothing has to cross between parts.
Inputs may be any that keep to these rules, and one draw needn't show every extreme that they name: `choices`: each row names 8 different experts. Among the 128 rows of one device every expert is named between 7 and 9 times, and one expert below 2 is named exactly 9 times by the rows of every device.
All inputs are finite; a program needn't handle non-finite values.
Results may differ from the reference program's by a relative error of at most 0.0085.
Values may be sent and summed in bfloat16 or wider, within the bound.
No kernel may reach another device: no remote copies, remote signals or barrier semaphores. Data moves between devices by JAX's collectives and lax.ppermute only.
A program may use at most 128 MiB of HBM per device.

```python
import math
import jax
import jax.numpy as jnp
from jax import lax

D = 2048
FF_WIN = 768
ALL_EXPERTS = 128
TOPK = 8
TOK_DEV = 128
SPLIT = 4
FH = 192
EXPERTS = 2
SLICES = 8
CAP = 9
TOKENS = 2048
N_DP = 2


def draw_choices(key, part):
    key = jax.random.fold_in(key, 11)
    blocks = TOKENS // TOK_DEV
    mean_count = TOK_DEV * TOPK // ALL_EXPERTS
    quarter = ALL_EXPERTS // 4
    hot_key, block_key = jax.random.split(key)
    hot_expert = jax.random.randint(hot_key, (), 0, EXPERTS)
    slot_ids = jnp.arange(TOK_DEV * TOPK, dtype=jnp.int32)
    expert_ids = jnp.arange(ALL_EXPERTS, dtype=jnp.int32)

    def one_block(sub_key):
        keys = jax.random.split(sub_key, 3)
        scores = jax.random.permutation(keys[0], ALL_EXPERTS).astype(jnp.int32)
        scores = jnp.where(expert_ids == hot_expert, -1, scores)
        ranking = jnp.argsort(jnp.argsort(scores))
        counts = mean_count + jnp.where(ranking < quarter, 1, jnp.where(ranking < 2 * quarter, -1, 0))
        bounds = jnp.cumsum(counts)
        expert_of = jnp.sum((bounds[None, :] <= slot_ids[:, None]).astype(jnp.int32), axis=1)
        table = expert_of.reshape(TOPK, TOK_DEV).T
        table = table[jax.random.permutation(keys[1], TOK_DEV)]
        shifts = jax.random.randint(keys[2], (TOK_DEV,), 0, TOPK)
        turned = (jnp.arange(TOPK, dtype=jnp.int32)[None, :] + shifts[:, None]) % TOPK
        return jnp.take_along_axis(table, turned, axis=1)
    tables = lax.map(one_block, jax.random.split(block_key, blocks))
    return tables.reshape(TOKENS, TOPK).astype(jnp.int32)


def level_of(stream_key, shape, pieces, least, largest):
    loudness = 1.0
    for position, shards_of in pieces:
        heights = jax.random.uniform(jax.random.fold_in(jax.random.fold_in(stream_key, 6), position), (shards_of,), jnp.float32, least / len(pieces), largest / len(pieces))
        loudness = loudness * jnp.repeat(jnp.exp(heights), shape[position] // shards_of).reshape((-1,) + (1,) * (len(shape) - 1 - position))
    return loudness


def scatter_about(rng, shape, width, most, cuts=(), kind=jnp.bfloat16):
    drawn = jax.random.normal(rng, shape, jnp.float32) * width
    if len(cuts) > 0:
        drawn = level_of(rng, shape, cuts, -0.22, 0.18) * drawn
    return jnp.clip(drawn, min=-most, max=most).astype(kind)


def setup_inputs(seed: int = 0, part: int = 0) -> dict:
    key_of = jax.random.split(jax.random.key(seed), 8)
    own_keys = jax.random.split(jax.random.fold_in(key_of[7], part), 8)
    return {
        "tokens": scatter_about(own_keys[0], (TOKENS, D), 1.0, 6.0, ((0, 16),)),
        "out_grad": scatter_about(own_keys[1], (TOKENS, D), 1.0, 6.0, ((0, 16),)),
        "choices": draw_choices(jax.random.fold_in(jax.random.fold_in(key_of[7], part), 71), part),
        "gates": jnp.clip(jnp.exp(math.log(1.0) - 2.9996462 * jax.random.uniform(own_keys[3], (TOKENS, TOPK), jnp.float32) ** level_of(own_keys[3], (TOKENS, TOPK), ((0, 16),), -0.2, 0.2)), 0.049804688, 1.0).astype(jnp.bfloat16),
        "gate_weight": scatter_about(key_of[4], (SLICES, D, FH), D ** -0.5, 0.125, ((0, 8),)),
        "up_weight": scatter_about(key_of[5], (SLICES, D, FH), D ** -0.5, 0.125, ((0, 8),)),
        "down_weight": scatter_about(key_of[6], (SLICES, FH, D), FF_WIN ** -0.5, 0.21875, ((0, 8),)),
    }


def silu_parts(pre_act):
    sigmoid = 1.0 / (1.0 + jnp.exp(-pre_act))
    return pre_act * sigmoid, sigmoid * (1.0 + pre_act * (1.0 - sigmoid))


def round_half(value):
    return lax.optimization_barrier(value.astype(jnp.bfloat16)).astype(jnp.float32)


def reference(tokens, out_grad, choices, gates, gate_weight, up_weight, down_weight):
    blocks = TOKENS // TOK_DEV
    flat_ids = choices.reshape(blocks, TOK_DEV * TOPK).astype(jnp.int32)
    flat_gates = gates.reshape(blocks, TOK_DEV * TOPK).astype(jnp.float32)
    window_ids = jnp.arange(EXPERTS, dtype=jnp.int32)
    hit_table = (flat_ids[:, :, None] == window_ids[None, None, :]).astype(jnp.int32)
    rank_in = jnp.sum((jnp.cumsum(hit_table, axis=1) - hit_table) * hit_table, axis=2).astype(jnp.int32)
    inside = flat_ids < EXPERTS
    expert_of = jnp.where(inside, flat_ids, EXPERTS).astype(jnp.int32)
    block_of = jnp.broadcast_to(jnp.arange(blocks, dtype=jnp.int32)[:, None], flat_ids.shape).astype(jnp.int32)
    token_of = (block_of * TOK_DEV + jnp.arange(TOK_DEV * TOPK, dtype=jnp.int32)[None, :] // TOPK).astype(jnp.int32)
    slot_tok = jnp.zeros((EXPERTS, blocks, CAP), jnp.int32).at[expert_of, block_of, rank_in].set(token_of, mode="drop")
    slot_gate = jnp.zeros((EXPERTS, blocks, CAP), jnp.float32).at[expert_of, block_of, rank_in].set(flat_gates, mode="drop")
    slot_live = jnp.zeros((EXPERTS, blocks, CAP), jnp.float32).at[expert_of, block_of, rank_in].set(1.0, mode="drop")

    def one_expert(expert):
        row_index = slot_tok[expert].reshape(-1)
        slot_used = slot_live[expert].reshape(-1)
        weight_of = slot_gate[expert].reshape(-1)
        input_rows = jnp.where(slot_used[:, None] > 0, tokens[row_index], jnp.zeros((), tokens.dtype)).astype(jnp.float32)
        grad_rows = jnp.where(slot_used[:, None] > 0, out_grad[row_index], jnp.zeros((), out_grad.dtype)).astype(jnp.float32)
        start = (expert * SPLIT).astype(jnp.int32)
        gate_slices = lax.dynamic_slice_in_dim(gate_weight, start, SPLIT, 0).astype(jnp.float32)
        up_slices = lax.dynamic_slice_in_dim(up_weight, start, SPLIT, 0).astype(jnp.float32)
        down_slices = lax.dynamic_slice_in_dim(down_weight, start, SPLIT, 0).astype(jnp.float32)
        pre_gate = jnp.einsum("rd,sdf->rsf", input_rows, gate_slices)
        pre_up = jnp.einsum("rd,sdf->rsf", input_rows, up_slices)
        silu_val, slope = silu_parts(pre_gate)
        activated = silu_val * pre_up
        back_grad = jnp.einsum("rd,sfd->rsf", grad_rows, down_slices)
        combine = jnp.sum(round_half(jnp.sum(back_grad * activated, axis=2)), axis=1)
        gated_back = weight_of[:, None, None] * back_grad
        scaled = round_half(weight_of[:, None, None] * activated)
        grad_gate_pre = round_half(gated_back * slope * pre_up)
        grad_up_pre = round_half(gated_back * silu_val)
        partial_value = jnp.einsum("rsf,sdf->rsd", grad_gate_pre, gate_slices) + jnp.einsum("rsf,sdf->rsd", grad_up_pre, up_slices)
        row_grad = jnp.sum(round_half(partial_value), axis=1)
        halves = blocks // N_DP
        input_rep = input_rows.reshape(halves, N_DP, CAP, D)
        grad_rep = grad_rows.reshape(halves, N_DP, CAP, D)
        gate_rep = grad_gate_pre.reshape(halves, N_DP, CAP, SPLIT, FH)
        up_rep = grad_up_pre.reshape(halves, N_DP, CAP, SPLIT, FH)
        scaled_rep = scaled.reshape(halves, N_DP, CAP, SPLIT, FH)
        gate_grad = jnp.sum(round_half(jnp.einsum("bncd,bncsf->nsdf", input_rep, gate_rep)), axis=0)
        up_grad = jnp.sum(round_half(jnp.einsum("bncd,bncsf->nsdf", input_rep, up_rep)), axis=0)
        down_grad = jnp.sum(round_half(jnp.einsum("bncsf,bncd->nsfd", scaled_rep, grad_rep)), axis=0)
        return row_grad, combine, gate_grad, up_grad, down_grad

    row_grads, combines, gate_grads, up_grads, down_grads = lax.map(one_expert, window_ids)
    in_grad = jnp.zeros((TOKENS, D), jnp.float32).at[slot_tok.reshape(-1)].add(row_grads.reshape(-1, D))
    picked = combines.reshape(EXPERTS, blocks, CAP)[jnp.minimum(expert_of, EXPERTS - 1), block_of, rank_in]
    combine_grad = jnp.where(inside, picked, jnp.zeros((), picked.dtype)).reshape(TOKENS, TOPK)
    return (in_grad.astype(jnp.bfloat16), combine_grad,
            gate_grads.reshape(SLICES, D, FH).astype(jnp.bfloat16),
            up_grads.reshape(SLICES, D, FH).astype(jnp.bfloat16),
            down_grads.reshape(SLICES, FH, D).astype(jnp.bfloat16))
```

```python
import jax
import jax.numpy as jnp
from jax import lax
from jax.experimental import pallas as pl
from jax.experimental.pallas import tpu as pltpu
from jax.sharding import PartitionSpec as P

SPLIT = 4
MAIN = 8
TILE = 128
GROUP = 8
VMEM_LIMIT = 60 * 1024 * 1024
F32 = jnp.float32
BF16 = jnp.bfloat16


def iota(shape, axis):
    return lax.broadcasted_iota(jnp.int32, shape, axis)


def dot(a, b, contract):
    return lax.dot_general(a, b, ((contract[:1], contract[1:]), ((), ())), preferred_element_type=F32)


def places(picks, expert):
    named = [jnp.any(picks == e, axis=0, keepdims=True) for e in expert]
    table = jnp.concatenate([n.astype(F32) for n in named], axis=0)
    count, toks = table.shape
    pad = -count % 8
    if pad:
        table = jnp.concatenate([table, jnp.zeros((pad, toks), F32)], axis=0)
    before = (iota((toks, toks), 0) < iota((toks, toks), 1)).astype(BF16)
    rank = dot(table.astype(BF16), before, (1, 0))
    rank = jnp.where(table > 0, rank, -1.0)
    return [rank[i : i + 1] for i in range(count)]


def pack_kernel(where_ref, picks_ref, gates_ref, tok_ref, grad_ref, *outs):
    window = len(outs)
    quad = where_ref[0]
    picks = picks_ref[...]
    gates = gates_ref[...].astype(F32)
    features = tok_ref.shape[1]
    fold = features // MAIN
    experts = [quad ^ k for k in range(window)]
    ranks = places(picks, experts)
    toks = picks.shape[1]
    seat = iota((MAIN, toks), 0).astype(F32)
    mains = [(r == seat).astype(F32) for r in ranks]
    last = jnp.concatenate([(r == float(MAIN)).astype(F32) for r in ranks], axis=0)
    pad = -window % 8
    if pad:
        last = jnp.concatenate([last, jnp.zeros((pad, toks), F32)], axis=0)
    choose = jnp.concatenate(mains + [last], axis=0).astype(BF16)
    tok_rows = dot(choose, tok_ref[...], (1, 0))
    grad_rows = dot(choose, grad_ref[...], (1, 0))
    row = iota((MAIN, fold), 0)
    lane = iota((MAIN, TILE), 1)
    for k, out in enumerate(outs):
        top = slice(k * MAIN, (k + 1) * MAIN)
        out[:, :features] = jnp.concatenate([tok_rows[top], grad_rows[top]], axis=0).astype(BF16)
        folded = []
        for rows in (tok_rows, grad_rows):
            at = window * MAIN + k
            total = jnp.zeros((MAIN, fold), F32)
            for c in range(MAIN):
                total = jnp.where(row == c, rows[at : at + 1, c * fold : (c + 1) * fold], total)
            folded.append(total)
        out[:, features : features + fold] = jnp.concatenate(folded, axis=0).astype(BF16)
        weight = jnp.sum(jnp.where(picks == experts[k], gates, 0.0), axis=0, keepdims=True)
        seat_gate = jnp.sum(mains[k] * weight, axis=1, keepdims=True)
        last_gate = jnp.sum(last[k : k + 1] * weight, axis=1, keepdims=True)
        tile = jnp.where(lane == 0, seat_gate, jnp.where(lane == 1, last_gate, 0.0))
        out[:, features + fold :] = jnp.concatenate([tile, tile], axis=0).astype(BF16)


def expert_kernel(
    where_ref, z0, z1, z2, z3, wg_ref, wu_ref, wd_ref, m0, m1, m2, m3, keep_ref, hid_ref, send_ref
):
    features = wg_ref.shape[1]
    hidden = wg_ref.shape[0]
    fold = features // MAIN
    half = features // 2
    core = where_ref[1]
    zs, ms = (z0, z1, z2, z3), (m0, m1, m2, m3)
    pair = 2 * MAIN
    per = GROUP // SPLIT
    rows_in = per * pair
    groups = z0.shape[0] // rows_in

    def work(g):
        if groups == 1:
            src = slice(0, rows_in)
            dst = slice(0, per * MAIN)
            all_rows = slice(0, (GROUP + 1) * pair)
        else:
            src = pl.ds(pl.multiple_of(g * rows_in, rows_in), rows_in)
            dst = pl.ds(pl.multiple_of(g * per * MAIN, per * MAIN), per * MAIN)
            all_rows = pl.ds(pl.multiple_of(g * (GROUP + 1) * pair, pair), (GROUP + 1) * pair)
        main = [z[src, :features] for z in zs]
        bent = jnp.concatenate([z[src, features : features + fold] for z in zs], axis=0)
        tiles = [z[src, features + fold :].astype(F32) for z in zs]
        n = GROUP * pair
        r, q = iota((n, n), 0), iota((n, n), 1)
        swap = ((r & 8) == (q & 8)) & ((r >> 4) == (q & 7)) & ((r & 7) == (q >> 4))
        flat = dot(swap.astype(BF16), bent, (1, 0)).astype(BF16)
        ninth = jnp.concatenate([flat[c * pair : (c + 1) * pair] for c in range(MAIN)], axis=1)
        rows = jnp.concatenate(main + [ninth], axis=0)
        pre_gate = dot(rows, wg_ref[...], (1, 1))
        pre_up = dot(rows, wu_ref[...], (1, 1))
        back = dot(rows, wd_ref[...], (1, 1))
        pieces = GROUP + 1
        upper = lambda v: v.reshape(pieces, 2, MAIN, hidden)[:, 0].reshape(pieces * MAIN, hidden)
        lower = lambda v: v.reshape(pieces, 2, MAIN, hidden)[:, 1].reshape(pieces * MAIN, hidden)
        pre_gate, pre_up, back = upper(pre_gate), upper(pre_up), lower(back)
        columns = []
        last = jnp.zeros((MAIN, 1), F32)
        seat = iota((MAIN, 1), 0)
        for p in range(GROUP):
            tile = tiles[p // per][(p % per) * pair : (p % per) * pair + MAIN]
            columns.append(tile[:, 0:1])
            last = jnp.where(seat == p, tile[:, 1:2], last)
        gate = jnp.concatenate(columns + [last], axis=0)
        sig = 1.0 / (1.0 + jnp.exp(-pre_gate))
        silu = pre_gate * sig
        slope = sig * (1.0 + pre_gate * (1.0 - sig))
        act = silu * pre_up
        combine = jnp.sum(back * act, axis=1, keepdims=True)
        scaled = gate * act
        gated = gate * back
        g_gate = (gated * slope * pre_up).astype(BF16)
        g_up = (gated * silu).astype(BF16)
        part = dot(g_gate, wg_ref[...], (1, 0)) + dot(g_up, wu_ref[...], (1, 0))
        tail = part[GROUP * MAIN :].astype(BF16).astype(F32)
        stack = jnp.concatenate([tail[:, c * fold : (c + 1) * fold] for c in range(MAIN)], axis=0)
        n = GROUP * MAIN
        r, q = iota((n, n), 0), iota((n, n), 1)
        turn = ((r >> 3) == (q & 7)) & ((r & 7) == (q >> 3))
        folded = dot(turn.astype(BF16), stack.astype(BF16), (1, 0))
        lane = iota((MAIN, TILE), 1)
        notes = []
        for p in range(GROUP):
            at = GROUP * MAIN + p
            notes.append(
                jnp.where(
                    lane == 0,
                    combine[p * MAIN : (p + 1) * MAIN],
                    jnp.where(lane == 1, combine[at : at + 1], 0.0),
                )
            )
        for j, m in enumerate(ms):
            span = slice(j * per * MAIN, (j + 1) * per * MAIN)
            m[dst, :features] = part[span].astype(BF16)
            m[dst, features : features + fold] = folded[span].astype(BF16)
            m[dst, features + fold :] = jnp.concatenate(
                notes[j * per : (j + 1) * per], axis=0
            ).astype(BF16)
        none = jnp.zeros((pieces, MAIN, hidden), F32)

        def lay(v, place):
            v = v.astype(F32).reshape(pieces, MAIN, hidden)
            both = [v, none] if place == 0 else [none, v]
            return jnp.stack(both, axis=1).reshape(pieces * 2 * MAIN, hidden).astype(BF16)

        hid = [lay(g_gate, 0), lay(g_up, 0), lay(scaled, 1)]
        low, high = rows[:, :half], rows[:, half:]
        keep_ref[all_rows, :] = jnp.where(core == 0, low, high)
        send_ref[all_rows, :half] = jnp.where(core == 0, high, low)
        for i, h in enumerate(hid):
            hid_ref[all_rows, i * hidden : (i + 1) * hidden] = h
            send_ref[all_rows, half + i * hidden : half + (i + 1) * hidden] = h

    if groups == 1:
        work(0)
    else:
        lax.fori_loop(0, groups, lambda g, c: (work(g), c)[1], 0)


def weights_kernel(keep_ref, hid_ref, peer_ref, gate_ref, up_ref, down_ref):
    half = keep_ref.shape[1]
    hidden = gate_ref.shape[0]
    outs = (gate_ref, up_ref, down_ref)
    for i, out in enumerate(outs):
        cols = slice(i * hidden, (i + 1) * hidden)
        far = slice(half + i * hidden, half + (i + 1) * hidden)
        total = dot(hid_ref[:, cols], keep_ref[...], (0, 0))
        total = total + dot(peer_ref[:, far], peer_ref[:, :half], (0, 0))
        out[...] = total.astype(BF16)


def finish_kernel(where_ref, picks_ref, o0, o1, o2, o3, *rest):
    far, (grad_ref, comb_ref) = rest[:-2], rest[-2:]
    window = 1 + len(far)
    quad = where_ref[0]
    picks = picks_ref[...]
    experts = [quad ^ k for k in range(window)]
    ranks = places(picks, experts)
    features = grad_ref.shape[1]
    fold = features // MAIN
    toks = picks.shape[1]
    seat = iota((MAIN, toks), 0).astype(F32)
    mains = [(r == seat).astype(F32) for r in ranks]
    lasts = [(r == float(MAIN)).astype(F32) for r in ranks]
    blocks = [(0, o[:MAIN, :].astype(F32)) for o in (o0, o1, o2, o3)]
    blocks += [(1 + k, f[...].astype(F32)) for k, f in enumerate(far)]
    row = iota((MAIN, toks), 0)
    for c in range(MAIN):
        cols = slice(c * fold, (c + 1) * fold)
        left, right = [], []
        for k, v in blocks:
            left += [mains[k], jnp.where(row == c, lasts[k], 0.0)]
            right += [v[:, cols], v[:, features : features + fold]]
        left = jnp.concatenate(left, axis=0).astype(BF16)
        right = jnp.concatenate(right, axis=0).astype(BF16)
        grad_ref[:, cols] = dot(left, right, (0, 0)).astype(BF16)
    terms = [jnp.zeros((1, toks), F32) for _ in range(window)]
    for k, v in blocks:
        note = v[:, features + fold :]
        terms[k] = terms[k] + jnp.sum(mains[k] * note[:, 0:1], axis=0, keepdims=True)
        terms[k] = terms[k] + lasts[k] * note[0:1, 1:2]
    comb = jnp.zeros(picks.shape, F32)
    for k in range(window):
        comb = comb + jnp.where(picks == experts[k], terms[k], 0.0)
    comb_ref[...] = comb


VM = pl.BlockSpec(memory_space=pltpu.VMEM)
SM = pl.BlockSpec(memory_space=pltpu.SMEM)


def call(kernel, outs, name, in_specs, flops, nbytes):
    return pl.pallas_call(
        kernel,
        out_shape=[jax.ShapeDtypeStruct(s, t) for s, t in outs],
        in_specs=in_specs,
        out_specs=[VM] * len(outs),
        compiler_params=pltpu.CompilerParams(vmem_limit_bytes=VMEM_LIMIT),
        cost_estimate=pl.CostEstimate(flops=flops, bytes_accessed=nbytes, transcendentals=0),
        name=name,
    )


def swap_by(block, mask):
    count = lax.axis_size("expert")
    return lax.ppermute(block, "expert", [(i, i ^ mask) for i in range(count)])


def body(tokens, out_grad, choices, gates, gate_weight, up_weight, down_weight):
    members = lax.axis_size("expert")
    position = lax.axis_index("expert")
    core = lax.axis_index("dp")
    toks, features = tokens.shape
    hidden = gate_weight.shape[2]
    window = members // SPLIT
    fold = features // MAIN
    half = features // 2
    width = features + fold + TILE
    where = jnp.stack([position // SPLIT, core]).astype(jnp.int32)
    picks, gates_t = choices.T, gates.T
    wg, wu, wd = gate_weight[0].T, up_weight[0].T, down_weight[0]

    packed = call(
        pack_kernel,
        [((2 * MAIN, width), BF16)] * window,
        "pack",
        [SM, VM, VM, VM, VM],
        2 * (MAIN + 1) * window * toks * features * 2,
        4 * toks * features,
    )(where, picks, gates_t, tokens, out_grad)
    own, others = packed[0], packed[1:]
    arrived = [swap_by(o, SPLIT * (k + 1)) for k, o in enumerate(others)]
    near = [own] + [swap_by(own, j) for j in range(1, SPLIT)]
    from_far = arrived[0] if window == 2 else jnp.concatenate(arrived, axis=0)
    far = [from_far] + [swap_by(from_far, j) for j in range(1, SPLIT)]
    zs = [jnp.concatenate([a, b], axis=0) for a, b in zip(near, far)]

    groups = members // GROUP
    all_rows = groups * (GROUP + 1) * 2 * MAIN
    *messages, keep, hid, send = call(
        expert_kernel,
        [((window * MAIN, width), BF16)] * SPLIT
        + [((all_rows, half), BF16), ((all_rows, 3 * hidden), BF16), ((all_rows, half + 3 * hidden), BF16)],
        "expert",
        [SM] + [VM] * 7,
        2 * all_rows * features * hidden * 5,
        6 * features * hidden,
    )(where, *zs, wg, wu, wd)
    back = [messages[0]] + [swap_by(messages[j], j) for j in range(1, SPLIT)]
    total = sum(b[MAIN:].astype(F32) for b in back).astype(BF16)
    homes = [
        swap_by(total[k * MAIN : (k + 1) * MAIN], SPLIT * (k + 1)) for k in range(window - 1)
    ]
    peer = lax.ppermute(send, "dp", [(0, 1), (1, 0)])
    gate_grad, up_grad, down_grad = call(
        weights_kernel,
        [((hidden, half), BF16)] * 3,
        "weights",
        [VM] * 3,
        2 * 2 * all_rows * half * hidden * 3,
        6 * half * hidden,
    )(keep, hid, peer)
    in_grad, combine = call(
        finish_kernel,
        [((toks, features), BF16), ((choices.shape[1], toks), F32)],
        "finish",
        [SM] + [VM] * (SPLIT + window),
        2 * toks * features * 16 * (SPLIT + window),
        2 * toks * features,
    )(where, picks, *back, *homes)
    return (
        in_grad,
        combine.T,
        gate_grad.T[None],
        up_grad.T[None],
        down_grad[None],
    )


def solution(mesh):
    return jax.shard_map(
        body,
        mesh=mesh,
        in_specs=(
            P(("groups", "expert", "dp"), None),
            P(("groups", "expert", "dp"), None),
            P(("groups", "expert", "dp"), None),
            P(("groups", "expert", "dp"), None),
            P("expert", None, None),
            P("expert", None, None),
            P("expert", None, None),
        ),
        out_specs=(
            P(("groups", "expert", "dp"), None),
            P(("groups", "expert", "dp"), None),
            P(("groups", "expert"), "dp", None),
            P(("groups", "expert"), "dp", None),
            P(("groups", "expert"), None, "dp"),
        ),
        check_vma=False,
    )
```

```python
import jax
import jax.numpy as jnp
from jax import lax
from jax.experimental import pallas as pl
from jax.experimental.pallas import tpu as pltpu
from jax.sharding import PartitionSpec as P

SPLIT = 4
MAIN = 8
TILE = 128
GROUP = 8
MIB = 1024 * 1024
VMEM_LIMIT = 60 * MIB
F32 = jnp.float32
BF16 = jnp.bfloat16


def iota(shape, axis):
    return lax.broadcasted_iota(jnp.int32, shape, axis)


def dot(a, b, contract):
    return lax.dot_general(a, b, ((contract[:1], contract[1:]), ((), ())), preferred_element_type=F32)


def places(picks, expert):
    named = [jnp.any(picks == e, axis=0, keepdims=True) for e in expert]
    table = jnp.concatenate([n.astype(F32) for n in named], axis=0)
    count, toks = table.shape
    pad = -count % 8
    if pad:
        table = jnp.concatenate([table, jnp.zeros((pad, toks), F32)], axis=0)
    before = (iota((toks, toks), 0) < iota((toks, toks), 1)).astype(BF16)
    rank = dot(table.astype(BF16), before, (1, 0))
    rank = jnp.where(table > 0, rank, -1.0)
    return [rank[i : i + 1] for i in range(count)]


def pack_kernel(picks_hbm, gates_hbm, tok_hbm, grad_hbm, *refs):
    outs, (picks_ref, gates_ref, tok_ref, grad_ref, sems) = refs[:-5], refs[-5:]
    loads = [
        pltpu.make_async_copy(src, dst, sems.at[i])
        for i, (src, dst) in enumerate(
            [(picks_hbm, picks_ref), (gates_hbm, gates_ref), (tok_hbm, tok_ref), (grad_hbm, grad_ref)]
        )
    ]
    for load in loads:
        load.start()
    window = len(outs)
    loads[0].wait()
    loads[1].wait()
    quad = lax.axis_index("expert") // SPLIT
    picks = picks_ref[...]
    gates = gates_ref[...].astype(F32)
    features = tok_ref.shape[1]
    fold = features // MAIN
    experts = [quad ^ k for k in range(window)]
    ranks = places(picks, experts)
    toks = picks.shape[1]
    seat = iota((MAIN, toks), 0).astype(F32)
    mains = [(r == seat).astype(F32) for r in ranks]
    last = jnp.concatenate([(r == float(MAIN)).astype(F32) for r in ranks], axis=0)
    pad = -window % 8
    if pad:
        last = jnp.concatenate([last, jnp.zeros((pad, toks), F32)], axis=0)
    choose = jnp.concatenate(mains + [last], axis=0).astype(BF16)
    loads[2].wait()
    tok_rows = dot(choose, tok_ref[...], (1, 0))
    loads[3].wait()
    grad_rows = dot(choose, grad_ref[...], (1, 0))
    row = iota((MAIN, fold), 0)
    lane = iota((MAIN, TILE), 1)
    for k, out in enumerate(outs):
        top = slice(k * MAIN, (k + 1) * MAIN)
        out[:, :features] = jnp.concatenate([tok_rows[top], grad_rows[top]], axis=0).astype(BF16)
        folded = []
        for rows in (tok_rows, grad_rows):
            at = window * MAIN + k
            total = jnp.zeros((MAIN, fold), F32)
            for c in range(MAIN):
                total = jnp.where(row == c, rows[at : at + 1, c * fold : (c + 1) * fold], total)
            folded.append(total)
        out[:, features : features + fold] = jnp.concatenate(folded, axis=0).astype(BF16)
        weight = jnp.sum(jnp.where(picks == experts[k], gates, 0.0), axis=0, keepdims=True)
        seat_gate = jnp.sum(mains[k] * weight, axis=1, keepdims=True)
        last_gate = jnp.sum(last[k : k + 1] * weight, axis=1, keepdims=True)
        tile = jnp.where(lane == 0, seat_gate, jnp.where(lane == 1, last_gate, 0.0))
        out[:, features + fold :] = jnp.concatenate([tile, tile], axis=0).astype(BF16)


def fetch_kernel(gate_hbm, up_hbm, down_hbm, *refs):
    outs, sems = refs[-4:-1], refs[-1]
    loads = [
        pltpu.make_async_copy(src, dst, sems.at[i])
        for i, (src, dst) in enumerate(zip((gate_hbm, up_hbm, down_hbm), outs))
    ]
    for load in loads:
        load.start()
    for load in loads:
        load.wait()


def expert_kernel(*refs):
    wg_ref, wu_ref, wd_ref, m0, m1, m2, m3, keep_ref, hid_ref, send_ref = refs[-10:]
    zs, ms = refs[:-10], (m0, m1, m2, m3)
    features = wg_ref.shape[1]
    hidden = wg_ref.shape[0]
    fold = features // MAIN
    half = features // 2
    core = lax.axis_index("dp")
    pair = 2 * MAIN
    per = GROUP // SPLIT
    held = GROUP // len(zs)
    rows_in = held * pair
    groups = zs[0].shape[0] // rows_in

    def work(g):
        if groups == 1:
            src = slice(0, rows_in)
            dst = slice(0, per * MAIN)
            all_rows = slice(0, (GROUP + 1) * pair)
        else:
            src = pl.ds(pl.multiple_of(g * rows_in, rows_in), rows_in)
            dst = pl.ds(pl.multiple_of(g * per * MAIN, per * MAIN), per * MAIN)
            all_rows = pl.ds(pl.multiple_of(g * (GROUP + 1) * pair, pair), (GROUP + 1) * pair)
        main = [z[src, :features] for z in zs]
        bent = jnp.concatenate([z[src, features : features + fold] for z in zs], axis=0)
        tiles = [z[src, features + fold :].astype(F32) for z in zs]
        n = GROUP * pair
        r, q = iota((n, n), 0), iota((n, n), 1)
        swap = ((r & 8) == (q & 8)) & ((r >> 4) == (q & 7)) & ((r & 7) == (q >> 4))
        flat = dot(swap.astype(BF16), bent, (1, 0)).astype(BF16)
        ninth = jnp.concatenate([flat[c * pair : (c + 1) * pair] for c in range(MAIN)], axis=1)
        rows = jnp.concatenate(main + [ninth], axis=0)
        pre_gate = dot(rows, wg_ref[...], (1, 1))
        pre_up = dot(rows, wu_ref[...], (1, 1))
        back = dot(rows, wd_ref[...], (1, 1))
        pieces = GROUP + 1
        upper = lambda v: v.reshape(pieces, 2, MAIN, hidden)[:, 0].reshape(pieces * MAIN, hidden)
        lower = lambda v: v.reshape(pieces, 2, MAIN, hidden)[:, 1].reshape(pieces * MAIN, hidden)
        pre_gate, pre_up, back = upper(pre_gate), upper(pre_up), lower(back)
        columns = []
        last = jnp.zeros((MAIN, 1), F32)
        seat = iota((MAIN, 1), 0)
        for p in range(GROUP):
            tile = tiles[p // held][(p % held) * pair : (p % held) * pair + MAIN]
            columns.append(tile[:, 0:1])
            last = jnp.where(seat == p, tile[:, 1:2], last)
        gate = jnp.concatenate(columns + [last], axis=0)
        sig = 1.0 / (1.0 + jnp.exp(-pre_gate))
        silu = pre_gate * sig
        slope = sig * (1.0 + pre_gate * (1.0 - sig))
        act = silu * pre_up
        combine = jnp.sum(back * act, axis=1, keepdims=True)
        scaled = gate * act
        gated = gate * back
        g_gate = (gated * slope * pre_up).astype(BF16)
        g_up = (gated * silu).astype(BF16)
        part = dot(g_gate, wg_ref[...], (1, 0)) + dot(g_up, wu_ref[...], (1, 0))
        tail = part[GROUP * MAIN :].astype(BF16).astype(F32)
        stack = jnp.concatenate([tail[:, c * fold : (c + 1) * fold] for c in range(MAIN)], axis=0)
        n = GROUP * MAIN
        r, q = iota((n, n), 0), iota((n, n), 1)
        turn = ((r >> 3) == (q & 7)) & ((r & 7) == (q >> 3))
        folded = dot(turn.astype(BF16), stack.astype(BF16), (1, 0))
        lane = iota((MAIN, TILE), 1)
        notes = []
        for p in range(GROUP):
            at = GROUP * MAIN + p
            notes.append(
                jnp.where(
                    lane == 0,
                    combine[p * MAIN : (p + 1) * MAIN],
                    jnp.where(lane == 1, combine[at : at + 1], 0.0),
                )
            )
        for j, m in enumerate(ms):
            span = slice(j * per * MAIN, (j + 1) * per * MAIN)
            m[dst, :features] = part[span].astype(BF16)
            m[dst, features : features + fold] = folded[span].astype(BF16)
            m[dst, features + fold :] = jnp.concatenate(
                notes[j * per : (j + 1) * per], axis=0
            ).astype(BF16)
        none = jnp.zeros((pieces, MAIN, hidden), F32)

        def lay(v, place):
            v = v.astype(F32).reshape(pieces, MAIN, hidden)
            both = [v, none] if place == 0 else [none, v]
            return jnp.stack(both, axis=1).reshape(pieces * 2 * MAIN, hidden).astype(BF16)

        hid = [lay(g_gate, 0), lay(g_up, 0), lay(scaled, 1)]
        low, high = rows[:, :half], rows[:, half:]
        keep_ref[all_rows, :] = jnp.where(core == 0, low, high)
        send_ref[all_rows, :half] = jnp.where(core == 0, high, low)
        for i, h in enumerate(hid):
            hid_ref[all_rows, i * hidden : (i + 1) * hidden] = h
            send_ref[all_rows, half + i * hidden : half + (i + 1) * hidden] = h

    if groups == 1:
        work(0)
    else:
        lax.fori_loop(0, groups, lambda g, c: (work(g), c)[1], 0)


def weights_kernel(keep_ref, hid_ref, peer_ref, gate_ref, up_ref, down_ref):
    half = keep_ref.shape[1]
    hidden = gate_ref.shape[0]
    outs = (gate_ref, up_ref, down_ref)
    for i, out in enumerate(outs):
        cols = slice(i * hidden, (i + 1) * hidden)
        far = slice(half + i * hidden, half + (i + 1) * hidden)
        total = dot(hid_ref[:, cols], keep_ref[...], (0, 0))
        total = total + dot(peer_ref[:, far], peer_ref[:, :half], (0, 0))
        out[...] = total.astype(BF16)


def finish_kernel(picks_ref, o0, o1, o2, o3, *rest):
    far, (grad_ref, comb_ref) = rest[:-2], rest[-2:]
    window = 1 + len(far)
    quad = lax.axis_index("expert") // SPLIT
    picks = picks_ref[...]
    experts = [quad ^ k for k in range(window)]
    ranks = places(picks, experts)
    features = grad_ref.shape[1]
    fold = features // MAIN
    toks = picks.shape[1]
    seat = iota((MAIN, toks), 0).astype(F32)
    mains = [(r == seat).astype(F32) for r in ranks]
    lasts = [(r == float(MAIN)).astype(F32) for r in ranks]
    blocks = [(0, o[:MAIN, :].astype(F32)) for o in (o0, o1, o2, o3)]
    blocks += [(1 + k, f[...].astype(F32)) for k, f in enumerate(far)]
    row = iota((MAIN, toks), 0)
    for c in range(MAIN):
        cols = slice(c * fold, (c + 1) * fold)
        left, right = [], []
        for k, v in blocks:
            left += [mains[k], jnp.where(row == c, lasts[k], 0.0)]
            right += [v[:, cols], v[:, features : features + fold]]
        left = jnp.concatenate(left, axis=0).astype(BF16)
        right = jnp.concatenate(right, axis=0).astype(BF16)
        grad_ref[:, cols] = dot(left, right, (0, 0)).astype(BF16)
    terms = [jnp.zeros((1, toks), F32) for _ in range(window)]
    for k, v in blocks:
        note = v[:, features + fold :]
        terms[k] = terms[k] + jnp.sum(mains[k] * note[:, 0:1], axis=0, keepdims=True)
        terms[k] = terms[k] + lasts[k] * note[0:1, 1:2]
    comb = jnp.zeros(picks.shape, F32)
    for k in range(window):
        comb = comb + jnp.where(picks == experts[k], terms[k], 0.0)
    comb_ref[...] = comb


VM = pl.BlockSpec(memory_space=pltpu.VMEM)
HBM = pl.BlockSpec(memory_space=pltpu.HBM)
ANY = pl.BlockSpec(memory_space=pl.ANY)


def call(kernel, outs, name, args, flops, nbytes, room, specs=None, scratch=()):
    specs = specs or [VM] * len(args)
    args = [
        pltpu.with_memory_space_constraint(a, pltpu.HBM) if s is HBM else a
        for a, s in zip(args, specs)
    ]
    return pl.pallas_call(
        kernel,
        out_shape=[jax.ShapeDtypeStruct(s, t) for s, t in outs],
        in_specs=specs,
        out_specs=[VM] * len(outs),
        scratch_shapes=list(scratch),
        compiler_params=pltpu.CompilerParams(vmem_limit_bytes=min(VMEM_LIMIT, room * MIB)),
        cost_estimate=pl.CostEstimate(flops=flops, bytes_accessed=nbytes, transcendentals=0),
        name=name,
    )(*args)


def swap_by(block, mask):
    count = lax.axis_size("expert")
    return lax.ppermute(block, "expert", [(i, i ^ mask) for i in range(count)])


def body(tokens, out_grad, choices, gates, gate_weight, up_weight, down_weight):
    members = lax.axis_size("expert")
    toks, features = tokens.shape
    hidden = gate_weight.shape[2]
    window = members // SPLIT
    fold = features // MAIN
    half = features // 2
    width = features + fold + TILE
    picks, gates_t = choices.T, gates.T
    wg, wu, wd = gate_weight[0].T, up_weight[0].T, down_weight[0]
    groups = members // GROUP

    packed = call(
        pack_kernel,
        [((2 * MAIN, width), BF16)] * window,
        "pack",
        (picks, gates_t, tokens, out_grad),
        2 * (MAIN + 1) * window * toks * features * 2,
        4 * toks * features,
        6 + window,
        [HBM] * 4,
        [pltpu.VMEM(v.shape, v.dtype) for v in (picks, gates_t, tokens, out_grad)]
        + [pltpu.SemaphoreType.DMA((4,))],
    )
    own, others = packed[0], packed[1:]
    arrived = [swap_by(o, SPLIT * (k + 1)) for k, o in enumerate(others)]
    near = [own] + [swap_by(own, j) for j in range(1, SPLIT)]
    held = call(
        fetch_kernel,
        [(w.shape, BF16) for w in (wg, wu, wd)],
        "fetch",
        (wg, wu, wd, *near[1:]),
        0,
        6 * features * hidden,
        4,
        [HBM] * 3 + [ANY] * (SPLIT - 1),
        [pltpu.SemaphoreType.DMA((3,))],
    )
    from_far = arrived[0] if window == 2 else jnp.concatenate(arrived, axis=0)
    far = [from_far] + [swap_by(from_far, j) for j in range(1, SPLIT)]
    pairs = list(zip(near, far))
    if groups == 1:
        zs = [z for pair in pairs for z in pair]
    else:
        zs = [jnp.concatenate(pair, axis=0) for pair in pairs]

    all_rows = groups * (GROUP + 1) * 2 * MAIN
    *messages, keep, hid, send = call(
        expert_kernel,
        [((window * MAIN, width), BF16)] * SPLIT
        + [((all_rows, half), BF16), ((all_rows, 3 * hidden), BF16), ((all_rows, half + 3 * hidden), BF16)],
        "expert",
        (*zs, *held),
        2 * all_rows * features * hidden * 5,
        6 * features * hidden,
        10 + 6 * groups,
    )
    back = [messages[0]] + [swap_by(messages[j], j) for j in range(1, SPLIT)]
    peer = lax.ppermute(send, "dp", [(0, 1), (1, 0)])
    gate_grad, up_grad, down_grad = call(
        weights_kernel,
        [((hidden, half), BF16)] * 3,
        "weights",
        (keep, hid, peer),
        2 * 2 * all_rows * half * hidden * 3,
        6 * half * hidden,
        6 + 2 * groups,
    )
    *back, gate_grad, up_grad, down_grad = lax.optimization_barrier(
        (*back, gate_grad, up_grad, down_grad)
    )
    total = sum(b[MAIN:].astype(F32) for b in back).astype(BF16)
    homes = [
        swap_by(total[k * MAIN : (k + 1) * MAIN], SPLIT * (k + 1)) for k in range(window - 1)
    ]
    in_grad, combine = call(
        finish_kernel,
        [((toks, features), BF16), ((choices.shape[1], toks), F32)],
        "finish",
        (picks, *back, *homes),
        2 * toks * features * 16 * (SPLIT + window),
        2 * toks * features,
        6 + window,
    )
    return (
        in_grad,
        combine.T,
        gate_grad.T[None],
        up_grad.T[None],
        down_grad[None],
    )


def solution(mesh):
    return jax.shard_map(
        body,
        mesh=mesh,
        in_specs=(
            P(("groups", "expert", "dp"), None),
            P(("groups", "expert", "dp"), None),
            P(("groups", "expert", "dp"), None),
            P(("groups", "expert", "dp"), None),
            P("expert", None, None),
            P("expert", None, None),
            P("expert", None, None),
        ),
        out_specs=(
            P(("groups", "expert", "dp"), None),
            P(("groups", "expert", "dp"), None),
            P(("groups", "expert"), "dp", None),
            P(("groups", "expert"), "dp", None),
            P(("groups", "expert"), None, "dp"),
        ),
        check_vma=False,
    )
```

```python
import jax
import jax.numpy as jnp
from jax import lax
from jax.experimental import pallas as pl
from jax.experimental.pallas import tpu as pltpu
from jax.sharding import PartitionSpec as P

SPLIT = 4
MAIN = 8
TILE = 128
GROUP = 8
MIB = 1024 * 1024
VMEM_LIMIT = 60 * MIB
F32 = jnp.float32
BF16 = jnp.bfloat16


def iota(shape, axis):
    return lax.broadcasted_iota(jnp.int32, shape, axis)


def dot(a, b, contract):
    return lax.dot_general(a, b, ((contract[:1], contract[1:]), ((), ())), preferred_element_type=F32)


def places(picks, expert):
    named = [jnp.any(picks == e, axis=0, keepdims=True) for e in expert]
    table = jnp.concatenate([n.astype(F32) for n in named], axis=0)
    count, toks = table.shape
    pad = -count % 8
    if pad:
        table = jnp.concatenate([table, jnp.zeros((pad, toks), F32)], axis=0)
    before = (iota((toks, toks), 0) < iota((toks, toks), 1)).astype(BF16)
    rank = dot(table.astype(BF16), before, (1, 0))
    rank = jnp.where(table > 0, rank, -1.0)
    return [rank[i : i + 1] for i in range(count)]


def pack_kernel(picks_hbm, gates_hbm, tok_hbm, grad_hbm, *refs):
    outs, (picks_ref, gates_ref, tok_ref, grad_ref, sems) = refs[:-5], refs[-5:]
    loads = [
        pltpu.make_async_copy(src, dst, sems.at[i])
        for i, (src, dst) in enumerate(
            [(picks_hbm, picks_ref), (gates_hbm, gates_ref), (tok_hbm, tok_ref), (grad_hbm, grad_ref)]
        )
    ]
    for load in loads:
        load.start()
    window = len(outs)
    loads[0].wait()
    loads[1].wait()
    quad = lax.axis_index("expert") // SPLIT
    picks = picks_ref[...]
    gates = gates_ref[...].astype(F32)
    features = tok_ref.shape[1]
    fold = features // MAIN
    experts = [quad ^ k for k in range(window)]
    ranks = places(picks, experts)
    toks = picks.shape[1]
    seat = iota((MAIN, toks), 0).astype(F32)
    mains = [(r == seat).astype(F32) for r in ranks]
    last = jnp.concatenate([(r == float(MAIN)).astype(F32) for r in ranks], axis=0)
    pad = -window % 8
    if pad:
        last = jnp.concatenate([last, jnp.zeros((pad, toks), F32)], axis=0)
    choose = jnp.concatenate(mains + [last], axis=0).astype(BF16)
    loads[2].wait()
    tok_rows = dot(choose, tok_ref[...], (1, 0))
    loads[3].wait()
    grad_rows = dot(choose, grad_ref[...], (1, 0))
    row = iota((MAIN, fold), 0)
    lane = iota((MAIN, TILE), 1)
    for k, out in enumerate(outs):
        top = slice(k * MAIN, (k + 1) * MAIN)
        out[:, :features] = jnp.concatenate([tok_rows[top], grad_rows[top]], axis=0).astype(BF16)
        folded = []
        for rows in (tok_rows, grad_rows):
            at = window * MAIN + k
            total = jnp.zeros((MAIN, fold), F32)
            for c in range(MAIN):
                total = jnp.where(row == c, rows[at : at + 1, c * fold : (c + 1) * fold], total)
            folded.append(total)
        out[:, features : features + fold] = jnp.concatenate(folded, axis=0).astype(BF16)
        weight = jnp.sum(jnp.where(picks == experts[k], gates, 0.0), axis=0, keepdims=True)
        seat_gate = jnp.sum(mains[k] * weight, axis=1, keepdims=True)
        last_gate = jnp.sum(last[k : k + 1] * weight, axis=1, keepdims=True)
        tile = jnp.where(lane == 0, seat_gate, jnp.where(lane == 1, last_gate, 0.0))
        out[:, features + fold :] = jnp.concatenate([tile, tile], axis=0).astype(BF16)


def fetch_kernel(gate_hbm, up_hbm, down_hbm, *refs):
    outs, sems = refs[-4:-1], refs[-1]
    loads = [
        pltpu.make_async_copy(src, dst, sems.at[i])
        for i, (src, dst) in enumerate(zip((gate_hbm, up_hbm, down_hbm), outs))
    ]
    for load in loads:
        load.start()
    for load in loads:
        load.wait()


def expert_kernel(*refs):
    wg_ref, wu_ref, wd_ref, m0, m1, m2, m3, keep_ref, hid_ref, send_ref = refs[-10:]
    zs, ms = refs[:-10], (m0, m1, m2, m3)
    features = wg_ref.shape[1]
    hidden = wg_ref.shape[0]
    fold = features // MAIN
    half = features // 2
    core = lax.axis_index("dp")
    pair = 2 * MAIN
    per = GROUP // SPLIT
    held = GROUP // len(zs)
    rows_in = held * pair
    groups = zs[0].shape[0] // rows_in

    def work(g):
        if groups == 1:
            src = slice(0, rows_in)
            dst = slice(0, per * MAIN)
            all_rows = slice(0, (GROUP + 1) * pair)
        else:
            src = pl.ds(pl.multiple_of(g * rows_in, rows_in), rows_in)
            dst = pl.ds(pl.multiple_of(g * per * MAIN, per * MAIN), per * MAIN)
            all_rows = pl.ds(pl.multiple_of(g * (GROUP + 1) * pair, pair), (GROUP + 1) * pair)
        main = [z[src, :features] for z in zs]
        bent = jnp.concatenate([z[src, features : features + fold] for z in zs], axis=0)
        tiles = [z[src, features + fold :].astype(F32) for z in zs]
        n = GROUP * pair
        r, q = iota((n, n), 0), iota((n, n), 1)
        swap = ((r & 8) == (q & 8)) & ((r >> 4) == (q & 7)) & ((r & 7) == (q >> 4))
        flat = dot(swap.astype(BF16), bent, (1, 0)).astype(BF16)
        ninth = jnp.concatenate([flat[c * pair : (c + 1) * pair] for c in range(MAIN)], axis=1)
        rows = jnp.concatenate(main + [ninth], axis=0)
        pre_gate = dot(rows, wg_ref[...], (1, 1))
        pre_up = dot(rows, wu_ref[...], (1, 1))
        back = dot(rows, wd_ref[...], (1, 1))
        pieces = GROUP + 1
        upper = lambda v: v.reshape(pieces, 2, MAIN, hidden)[:, 0].reshape(pieces * MAIN, hidden)
        lower = lambda v: v.reshape(pieces, 2, MAIN, hidden)[:, 1].reshape(pieces * MAIN, hidden)
        pre_gate, pre_up, back = upper(pre_gate), upper(pre_up), lower(back)
        columns = []
        last = jnp.zeros((MAIN, 1), F32)
        seat = iota((MAIN, 1), 0)
        for p in range(GROUP):
            tile = tiles[p // held][(p % held) * pair : (p % held) * pair + MAIN]
            columns.append(tile[:, 0:1])
            last = jnp.where(seat == p, tile[:, 1:2], last)
        gate = jnp.concatenate(columns + [last], axis=0)
        sig = 1.0 / (1.0 + jnp.exp(-pre_gate))
        silu = pre_gate * sig
        slope = sig * (1.0 + pre_gate * (1.0 - sig))
        act = silu * pre_up
        combine = jnp.sum(back * act, axis=1, keepdims=True)
        scaled = gate * act
        gated = gate * back
        g_gate = (gated * slope * pre_up).astype(BF16)
        g_up = (gated * silu).astype(BF16)
        part = dot(g_gate, wg_ref[...], (1, 0)) + dot(g_up, wu_ref[...], (1, 0))
        tail = part[GROUP * MAIN :].astype(BF16).astype(F32)
        stack = jnp.concatenate([tail[:, c * fold : (c + 1) * fold] for c in range(MAIN)], axis=0)
        n = GROUP * MAIN
        r, q = iota((n, n), 0), iota((n, n), 1)
        turn = ((r >> 3) == (q & 7)) & ((r & 7) == (q >> 3))
        folded = dot(turn.astype(BF16), stack.astype(BF16), (1, 0))
        lane = iota((MAIN, TILE), 1)
        notes = []
        for p in range(GROUP):
            at = GROUP * MAIN + p
            notes.append(
                jnp.where(
                    lane == 0,
                    combine[p * MAIN : (p + 1) * MAIN],
                    jnp.where(lane == 1, combine[at : at + 1], 0.0),
                )
            )
        for j, m in enumerate(ms):
            span = slice(j * per * MAIN, (j + 1) * per * MAIN)
            m[dst, :features] = part[span].astype(BF16)
            m[dst, features : features + fold] = folded[span].astype(BF16)
            m[dst, features + fold :] = jnp.concatenate(
                notes[j * per : (j + 1) * per], axis=0
            ).astype(BF16)
        none = jnp.zeros((pieces, MAIN, hidden), F32)

        def lay(v, place):
            v = v.astype(F32).reshape(pieces, MAIN, hidden)
            both = [v, none] if place == 0 else [none, v]
            return jnp.stack(both, axis=1).reshape(pieces * 2 * MAIN, hidden).astype(BF16)

        hid = [lay(g_gate, 0), lay(g_up, 0), lay(scaled, 1)]
        low, high = rows[:, :half], rows[:, half:]
        keep_ref[all_rows, :] = jnp.where(core == 0, low, high)
        send_ref[all_rows, :half] = jnp.where(core == 0, high, low)
        for i, h in enumerate(hid):
            hid_ref[all_rows, i * hidden : (i + 1) * hidden] = h
            send_ref[all_rows, half + i * hidden : half + (i + 1) * hidden] = h

    if groups == 1:
        work(0)
    else:
        lax.fori_loop(0, groups, lambda g, c: (work(g), c)[1], 0)


def weights_kernel(keep_ref, hid_ref, peer_ref, gate_ref, up_ref, down_ref):
    half = keep_ref.shape[1]
    hidden = gate_ref.shape[0]
    outs = (gate_ref, up_ref, down_ref)
    for i, out in enumerate(outs):
        cols = slice(i * hidden, (i + 1) * hidden)
        far = slice(half + i * hidden, half + (i + 1) * hidden)
        total = dot(hid_ref[:, cols], keep_ref[...], (0, 0))
        total = total + dot(peer_ref[:, far], peer_ref[:, :half], (0, 0))
        out[...] = total.astype(BF16)


def finish_kernel(picks_ref, o0, o1, o2, o3, *rest):
    far, (grad_ref, comb_ref) = rest[:-2], rest[-2:]
    window = 1 + len(far)
    quad = lax.axis_index("expert") // SPLIT
    picks = picks_ref[...]
    experts = [quad ^ k for k in range(window)]
    ranks = places(picks, experts)
    features = grad_ref.shape[1]
    fold = features // MAIN
    toks = picks.shape[1]
    seat = iota((MAIN, toks), 0).astype(F32)
    mains = [(r == seat).astype(F32) for r in ranks]
    lasts = [(r == float(MAIN)).astype(F32) for r in ranks]
    blocks = [(0, o[:MAIN, :].astype(F32)) for o in (o0, o1, o2, o3)]
    blocks += [(1 + k, f[...].astype(F32)) for k, f in enumerate(far)]
    row = iota((MAIN, toks), 0)
    for c in range(MAIN):
        cols = slice(c * fold, (c + 1) * fold)
        left, right = [], []
        for k, v in blocks:
            left += [mains[k], jnp.where(row == c, lasts[k], 0.0)]
            right += [v[:, cols], v[:, features : features + fold]]
        left = jnp.concatenate(left, axis=0).astype(BF16)
        right = jnp.concatenate(right, axis=0).astype(BF16)
        grad_ref[:, cols] = dot(left, right, (0, 0)).astype(BF16)
    terms = [jnp.zeros((1, toks), F32) for _ in range(window)]
    for k, v in blocks:
        note = v[:, features + fold :]
        terms[k] = terms[k] + jnp.sum(mains[k] * note[:, 0:1], axis=0, keepdims=True)
        terms[k] = terms[k] + lasts[k] * note[0:1, 1:2]
    comb = jnp.zeros(picks.shape, F32)
    for k in range(window):
        comb = comb + jnp.where(picks == experts[k], terms[k], 0.0)
    comb_ref[...] = comb


VM = pl.BlockSpec(memory_space=pltpu.VMEM)
HBM = pl.BlockSpec(memory_space=pltpu.HBM)
ANY = pl.BlockSpec(memory_space=pl.ANY)


def call(kernel, outs, name, args, flops, nbytes, room, specs=None, scratch=()):
    specs = specs or [VM] * len(args)
    args = [
        pltpu.with_memory_space_constraint(a, pltpu.HBM) if s is HBM else a
        for a, s in zip(args, specs)
    ]
    return pl.pallas_call(
        kernel,
        out_shape=[jax.ShapeDtypeStruct(s, t) for s, t in outs],
        in_specs=specs,
        out_specs=[VM] * len(outs),
        scratch_shapes=list(scratch),
        compiler_params=pltpu.CompilerParams(vmem_limit_bytes=min(VMEM_LIMIT, room * MIB)),
        cost_estimate=pl.CostEstimate(flops=flops, bytes_accessed=nbytes, transcendentals=0),
        name=name,
    )(*args)


def swap_by(block, mask):
    count = lax.axis_size("expert")
    return lax.ppermute(block, "expert", [(i, i ^ mask) for i in range(count)])


def body(tokens, out_grad, choices, gates, gate_weight, up_weight, down_weight):
    members = lax.axis_size("expert")
    toks, features = tokens.shape
    hidden = gate_weight.shape[2]
    window = members // SPLIT
    fold = features // MAIN
    half = features // 2
    width = features + fold + TILE
    picks, gates_t = choices.T, gates.T
    wg, wu, wd = gate_weight[0].T, up_weight[0].T, down_weight[0]
    groups = members // GROUP

    packed = call(
        pack_kernel,
        [((2 * MAIN, width), BF16)] * window,
        "pack",
        (picks, gates_t, tokens, out_grad),
        2 * (MAIN + 1) * window * toks * features * 2,
        4 * toks * features,
        6 + window,
        [HBM] * 4,
        [pltpu.VMEM(v.shape, v.dtype) for v in (picks, gates_t, tokens, out_grad)]
        + [pltpu.SemaphoreType.DMA((4,))],
    )
    own, others = packed[0], packed[1:]
    arrived = [swap_by(o, SPLIT * (k + 1)) for k, o in enumerate(others)]
    near = [own] + [swap_by(own, j) for j in range(1, SPLIT)]
    held = call(
        fetch_kernel,
        [(w.shape, BF16) for w in (wg, wu, wd)],
        "fetch",
        (wg, wu, wd, *near[1:]),
        0,
        6 * features * hidden,
        4,
        [HBM] * 3 + [ANY] * (SPLIT - 1),
        [pltpu.SemaphoreType.DMA((3,))],
    )
    from_far = arrived[0] if window == 2 else jnp.concatenate(arrived, axis=0)
    far = [from_far] + [swap_by(from_far, j) for j in range(1, SPLIT)]
    pairs = list(zip(near, far))
    if groups == 1:
        zs = [z for pair in pairs for z in pair]
    else:
        zs = [jnp.concatenate(pair, axis=0) for pair in pairs]

    all_rows = groups * (GROUP + 1) * 2 * MAIN
    *messages, keep, hid, send = call(
        expert_kernel,
        [((window * MAIN, width), BF16)] * SPLIT
        + [((all_rows, half), BF16), ((all_rows, 3 * hidden), BF16), ((all_rows, half + 3 * hidden), BF16)],
        "expert",
        (*zs, *held),
        2 * all_rows * features * hidden * 5,
        6 * features * hidden,
        10 + 6 * groups,
    )
    back = [messages[0]] + [swap_by(messages[j], j) for j in range(1, SPLIT)]
    peer = lax.ppermute(send, "dp", [(0, 1), (1, 0)])
    gate_grad, up_grad, down_grad = call(
        weights_kernel,
        [((hidden, half), BF16)] * 3,
        "weights",
        (keep, hid, peer),
        2 * 2 * all_rows * half * hidden * 3,
        6 * half * hidden,
        6 + 2 * groups,
    )
    gate_grad, up_grad, down_grad, *back = lax.optimization_barrier(
        (gate_grad, up_grad, down_grad, *back[::-1])
    )
    back = back[::-1]
    total = sum(b[MAIN:].astype(F32) for b in back).astype(BF16)
    homes = [
        swap_by(total[k * MAIN : (k + 1) * MAIN], SPLIT * (k + 1)) for k in range(window - 1)
    ]
    in_grad, combine = call(
        finish_kernel,
        [((toks, features), BF16), ((choices.shape[1], toks), F32)],
        "finish",
        (picks, *back, *homes),
        2 * toks * features * 16 * (SPLIT + window),
        2 * toks * features,
        6 + window,
    )
    return (
        in_grad,
        combine.T,
        gate_grad.T[None],
        up_grad.T[None],
        down_grad[None],
    )


def solution(mesh):
    return jax.shard_map(
        body,
        mesh=mesh,
        in_specs=(
            P(("groups", "expert", "dp"), None),
            P(("groups", "expert", "dp"), None),
            P(("groups", "expert", "dp"), None),
            P(("groups", "expert", "dp"), None),
            P("expert", None, None),
            P("expert", None, None),
            P("expert", None, None),
        ),
        out_specs=(
            P(("groups", "expert", "dp"), None),
            P(("groups", "expert", "dp"), None),
            P(("groups", "expert"), "dp", None),
            P(("groups", "expert"), "dp", None),
            P(("groups", "expert"), None, "dp"),
        ),
        check_vma=False,
    )
```

```python
import jax
import jax.numpy as jnp
from jax import lax
from jax.experimental import pallas as pl
from jax.experimental.pallas import tpu as pltpu
from jax.sharding import PartitionSpec as P

SPLIT = 4
MAIN = 8
TILE = 128
GROUP = 8
MIB = 1024 * 1024
VMEM_LIMIT = 60 * MIB
F32 = jnp.float32
BF16 = jnp.bfloat16


def iota(shape, axis):
    return lax.broadcasted_iota(jnp.int32, shape, axis)


def dot(a, b, contract):
    return lax.dot_general(a, b, ((contract[:1], contract[1:]), ((), ())), preferred_element_type=F32)


def places(picks, expert):
    named = [jnp.any(picks == e, axis=0, keepdims=True) for e in expert]
    table = jnp.concatenate([n.astype(F32) for n in named], axis=0)
    count, toks = table.shape
    pad = -count % 8
    if pad:
        table = jnp.concatenate([table, jnp.zeros((pad, toks), F32)], axis=0)
    before = (iota((toks, toks), 0) < iota((toks, toks), 1)).astype(BF16)
    rank = dot(table.astype(BF16), before, (1, 0))
    return jnp.where(table > 0, rank, -1.0)


def pack_kernel(picks_hbm, gates_hbm, tok_hbm, grad_hbm, *refs):
    outs, rank_ref = refs[:-6], refs[-6]
    picks_ref, gates_ref, tok_ref, grad_ref, sems = refs[-5:]
    loads = [
        pltpu.make_async_copy(src, dst, sems.at[i])
        for i, (src, dst) in enumerate(
            [(picks_hbm, picks_ref), (gates_hbm, gates_ref), (tok_hbm, tok_ref), (grad_hbm, grad_ref)]
        )
    ]
    for load in loads:
        load.start()
    window = len(outs)
    loads[0].wait()
    loads[1].wait()
    quad = lax.axis_index("expert") // SPLIT
    picks = picks_ref[...]
    gates = gates_ref[...].astype(F32)
    features = tok_ref.shape[1]
    fold = features // MAIN
    experts = [quad ^ k for k in range(window)]
    table = places(picks, experts)
    rank_ref[...] = table
    ranks = [table[k : k + 1] for k in range(window)]
    toks = picks.shape[1]
    seat = iota((MAIN, toks), 0).astype(F32)
    mains = [(r == seat).astype(F32) for r in ranks]
    last = jnp.concatenate([(r == float(MAIN)).astype(F32) for r in ranks], axis=0)
    pad = -window % 8
    if pad:
        last = jnp.concatenate([last, jnp.zeros((pad, toks), F32)], axis=0)
    choose = jnp.concatenate(mains + [last], axis=0).astype(BF16)
    loads[2].wait()
    tok_rows = dot(choose, tok_ref[...], (1, 0))
    loads[3].wait()
    grad_rows = dot(choose, grad_ref[...], (1, 0))
    row = iota((MAIN, fold), 0)
    lane = iota((MAIN, TILE), 1)
    for k, out in enumerate(outs):
        top = slice(k * MAIN, (k + 1) * MAIN)
        out[:, :features] = jnp.concatenate([tok_rows[top], grad_rows[top]], axis=0).astype(BF16)
        folded = []
        for rows in (tok_rows, grad_rows):
            at = window * MAIN + k
            total = jnp.zeros((MAIN, fold), F32)
            for c in range(MAIN):
                total = jnp.where(row == c, rows[at : at + 1, c * fold : (c + 1) * fold], total)
            folded.append(total)
        out[:, features : features + fold] = jnp.concatenate(folded, axis=0).astype(BF16)
        weight = jnp.sum(jnp.where(picks == experts[k], gates, 0.0), axis=0, keepdims=True)
        seat_gate = jnp.sum(mains[k] * weight, axis=1, keepdims=True)
        last_gate = jnp.sum(last[k : k + 1] * weight, axis=1, keepdims=True)
        tile = jnp.where(lane == 0, seat_gate, jnp.where(lane == 1, last_gate, 0.0))
        out[:, features + fold :] = jnp.concatenate([tile, tile], axis=0).astype(BF16)


def fetch_kernel(gate_hbm, up_hbm, down_hbm, *refs):
    outs, sems = refs[-4:-1], refs[-1]
    loads = [
        pltpu.make_async_copy(src, dst, sems.at[i])
        for i, (src, dst) in enumerate(zip((gate_hbm, up_hbm, down_hbm), outs))
    ]
    for load in loads:
        load.start()
    for load in loads:
        load.wait()


def expert_kernel(*refs):
    wg_ref, wu_ref, wd_ref, m0, m1, m2, m3, keep_ref, hid_ref, send_ref = refs[-10:]
    zs, ms = refs[:-10], (m0, m1, m2, m3)
    features = wg_ref.shape[1]
    hidden = wg_ref.shape[0]
    fold = features // MAIN
    half = features // 2
    core = lax.axis_index("dp")
    pair = 2 * MAIN
    per = GROUP // SPLIT
    held = GROUP // len(zs)
    rows_in = held * pair
    groups = zs[0].shape[0] // rows_in

    def work(g):
        if groups == 1:
            src = slice(0, rows_in)
            dst = slice(0, per * MAIN)
            all_rows = slice(0, (GROUP + 1) * pair)
        else:
            src = pl.ds(pl.multiple_of(g * rows_in, rows_in), rows_in)
            dst = pl.ds(pl.multiple_of(g * per * MAIN, per * MAIN), per * MAIN)
            all_rows = pl.ds(pl.multiple_of(g * (GROUP + 1) * pair, pair), (GROUP + 1) * pair)
        main = [z[src, :features] for z in zs]
        bent = jnp.concatenate([z[src, features : features + fold] for z in zs], axis=0)
        tiles = [z[src, features + fold :].astype(F32) for z in zs]
        n = GROUP * pair
        r, q = iota((n, n), 0), iota((n, n), 1)
        swap = ((r & 8) == (q & 8)) & ((r >> 4) == (q & 7)) & ((r & 7) == (q >> 4))
        flat = dot(swap.astype(BF16), bent, (1, 0)).astype(BF16)
        ninth = jnp.concatenate([flat[c * pair : (c + 1) * pair] for c in range(MAIN)], axis=1)
        rows = jnp.concatenate(main + [ninth], axis=0)
        pre_gate = dot(rows, wg_ref[...], (1, 1))
        pre_up = dot(rows, wu_ref[...], (1, 1))
        back = dot(rows, wd_ref[...], (1, 1))
        pieces = GROUP + 1
        upper = lambda v: v.reshape(pieces, 2, MAIN, hidden)[:, 0].reshape(pieces * MAIN, hidden)
        lower = lambda v: v.reshape(pieces, 2, MAIN, hidden)[:, 1].reshape(pieces * MAIN, hidden)
        pre_gate, pre_up, back = upper(pre_gate), upper(pre_up), lower(back)
        columns = []
        last = jnp.zeros((MAIN, 1), F32)
        seat = iota((MAIN, 1), 0)
        for p in range(GROUP):
            tile = tiles[p // held][(p % held) * pair : (p % held) * pair + MAIN]
            columns.append(tile[:, 0:1])
            last = jnp.where(seat == p, tile[:, 1:2], last)
        gate = jnp.concatenate(columns + [last], axis=0)
        sig = 1.0 / (1.0 + jnp.exp(-pre_gate))
        silu = pre_gate * sig
        slope = sig * (1.0 + pre_gate * (1.0 - sig))
        act = silu * pre_up
        combine = jnp.sum(back * act, axis=1, keepdims=True)
        scaled = gate * act
        gated = gate * back
        g_gate = (gated * slope * pre_up).astype(BF16)
        g_up = (gated * silu).astype(BF16)
        part = dot(g_gate, wg_ref[...], (1, 0)) + dot(g_up, wu_ref[...], (1, 0))
        tail = part[GROUP * MAIN :].astype(BF16).astype(F32)
        stack = jnp.concatenate([tail[:, c * fold : (c + 1) * fold] for c in range(MAIN)], axis=0)
        n = GROUP * MAIN
        r, q = iota((n, n), 0), iota((n, n), 1)
        turn = ((r >> 3) == (q & 7)) & ((r & 7) == (q >> 3))
        folded = dot(turn.astype(BF16), stack.astype(BF16), (1, 0))
        lane = iota((MAIN, TILE), 1)
        notes = []
        for p in range(GROUP):
            at = GROUP * MAIN + p
            notes.append(
                jnp.where(
                    lane == 0,
                    combine[p * MAIN : (p + 1) * MAIN],
                    jnp.where(lane == 1, combine[at : at + 1], 0.0),
                )
            )
        for j, m in enumerate(ms):
            span = slice(j * per * MAIN, (j + 1) * per * MAIN)
            m[dst, :features] = part[span].astype(BF16)
            m[dst, features : features + fold] = folded[span].astype(BF16)
            m[dst, features + fold :] = jnp.concatenate(
                notes[j * per : (j + 1) * per], axis=0
            ).astype(BF16)
        none = jnp.zeros((pieces, MAIN, hidden), F32)

        def lay(v, place):
            v = v.astype(F32).reshape(pieces, MAIN, hidden)
            both = [v, none] if place == 0 else [none, v]
            return jnp.stack(both, axis=1).reshape(pieces * 2 * MAIN, hidden).astype(BF16)

        hid = [lay(g_gate, 0), lay(g_up, 0), lay(scaled, 1)]
        low, high = rows[:, :half], rows[:, half:]
        keep_ref[all_rows, :] = jnp.where(core == 0, low, high)
        send_ref[all_rows, :half] = jnp.where(core == 0, high, low)
        for i, h in enumerate(hid):
            hid_ref[all_rows, i * hidden : (i + 1) * hidden] = h
            send_ref[all_rows, half + i * hidden : half + (i + 1) * hidden] = h

    if groups == 1:
        work(0)
    else:
        lax.fori_loop(0, groups, lambda g, c: (work(g), c)[1], 0)


def weights_kernel(keep_ref, hid_ref, peer_ref, gate_ref, up_ref, down_ref):
    half = keep_ref.shape[1]
    hidden = gate_ref.shape[0]
    outs = (gate_ref, up_ref, down_ref)
    for i, out in enumerate(outs):
        cols = slice(i * hidden, (i + 1) * hidden)
        far = slice(half + i * hidden, half + (i + 1) * hidden)
        total = dot(hid_ref[:, cols], keep_ref[...], (0, 0))
        total = total + dot(peer_ref[:, far], peer_ref[:, :half], (0, 0))
        out[...] = total.astype(BF16)


def finish_kernel(picks_ref, rank_ref, o0, o1, o2, o3, *rest):
    far, (grad_hbm, comb_ref, grad_ref, sems) = rest[:-4], rest[-4:]
    window = 1 + len(far)
    quad = lax.axis_index("expert") // SPLIT
    picks = picks_ref[...]
    experts = [quad ^ k for k in range(window)]
    ranks = [rank_ref[k : k + 1, :] for k in range(window)]
    features = grad_ref.shape[1]
    fold = features // MAIN
    toks = picks.shape[1]
    seat = iota((MAIN, toks), 0).astype(F32)
    mains = [(r == seat).astype(F32) for r in ranks]
    lasts = [(r == float(MAIN)).astype(F32) for r in ranks]
    blocks = [(0, o[:MAIN, :].astype(F32)) for o in (o0, o1, o2, o3)]
    blocks += [(1 + k, f[...].astype(F32)) for k, f in enumerate(far)]
    row = iota((MAIN, toks), 0)
    stores = []
    for c in range(MAIN):
        cols = slice(c * fold, (c + 1) * fold)
        left, right = [], []
        for k, v in blocks:
            left += [mains[k], jnp.where(row == c, lasts[k], 0.0)]
            right += [v[:, cols], v[:, features : features + fold]]
        left = jnp.concatenate(left, axis=0).astype(BF16)
        right = jnp.concatenate(right, axis=0).astype(BF16)
        grad_ref[:, cols] = dot(left, right, (0, 0)).astype(BF16)
        if c % 2:
            both = slice((c - 1) * fold, (c + 1) * fold)
            store = pltpu.make_async_copy(
                grad_ref.at[:, both], grad_hbm.at[:, both], sems.at[c // 2]
            )
            store.start()
            stores.append(store)
    terms = [jnp.zeros((1, toks), F32) for _ in range(window)]
    for k, v in blocks:
        note = v[:, features + fold :]
        terms[k] = terms[k] + jnp.sum(mains[k] * note[:, 0:1], axis=0, keepdims=True)
        terms[k] = terms[k] + lasts[k] * note[0:1, 1:2]
    comb = jnp.zeros(picks.shape, F32)
    for k in range(window):
        comb = comb + jnp.where(picks == experts[k], terms[k], 0.0)
    comb_ref[...] = comb
    for store in stores:
        store.wait()


VM = pl.BlockSpec(memory_space=pltpu.VMEM)
HBM = pl.BlockSpec(memory_space=pltpu.HBM)
ANY = pl.BlockSpec(memory_space=pl.ANY)


def call(kernel, outs, name, args, flops, nbytes, room, specs=None, scratch=(), out_specs=None):
    specs = specs or [VM] * len(args)
    args = [
        pltpu.with_memory_space_constraint(a, pltpu.HBM) if s is HBM else a
        for a, s in zip(args, specs)
    ]
    return pl.pallas_call(
        kernel,
        out_shape=[jax.ShapeDtypeStruct(s, t) for s, t in outs],
        in_specs=specs,
        out_specs=out_specs or [VM] * len(outs),
        scratch_shapes=list(scratch),
        compiler_params=pltpu.CompilerParams(vmem_limit_bytes=min(VMEM_LIMIT, room * MIB)),
        cost_estimate=pl.CostEstimate(flops=flops, bytes_accessed=nbytes, transcendentals=0),
        name=name,
    )(*args)


def swap_by(block, mask):
    count = lax.axis_size("expert")
    return lax.ppermute(block, "expert", [(i, i ^ mask) for i in range(count)])


def body(tokens, out_grad, choices, gates, gate_weight, up_weight, down_weight):
    members = lax.axis_size("expert")
    toks, features = tokens.shape
    hidden = gate_weight.shape[2]
    window = members // SPLIT
    fold = features // MAIN
    half = features // 2
    width = features + fold + TILE
    picks, gates_t = choices.T, gates.T
    wg, wu, wd = gate_weight[0].T, up_weight[0].T, down_weight[0]
    groups = members // GROUP

    *packed, ranks = call(
        pack_kernel,
        [((2 * MAIN, width), BF16)] * window + [((-(-window // 8) * 8, toks), F32)],
        "pack",
        (picks, gates_t, tokens, out_grad),
        2 * (MAIN + 1) * window * toks * features * 2,
        4 * toks * features,
        6 + window,
        [HBM] * 4,
        [pltpu.VMEM(v.shape, v.dtype) for v in (picks, gates_t, tokens, out_grad)]
        + [pltpu.SemaphoreType.DMA((4,))],
    )
    own, others = packed[0], packed[1:]
    arrived = [swap_by(o, SPLIT * (k + 1)) for k, o in enumerate(others)]
    near = [own] + [swap_by(own, j) for j in range(1, SPLIT)]
    held = call(
        fetch_kernel,
        [(w.shape, BF16) for w in (wg, wu, wd)],
        "fetch",
        (wg, wu, wd, *near[1:]),
        0,
        6 * features * hidden,
        4,
        [HBM] * 3 + [ANY] * (SPLIT - 1),
        [pltpu.SemaphoreType.DMA((3,))],
    )
    from_far = arrived[0] if window == 2 else jnp.concatenate(arrived, axis=0)
    far = [from_far] + [swap_by(from_far, j) for j in range(1, SPLIT)]
    pairs = list(zip(near, far))
    if groups == 1:
        zs = [z for pair in pairs for z in pair]
    else:
        zs = [jnp.concatenate(pair, axis=0) for pair in pairs]

    all_rows = groups * (GROUP + 1) * 2 * MAIN
    *messages, keep, hid, send = call(
        expert_kernel,
        [((window * MAIN, width), BF16)] * SPLIT
        + [((all_rows, half), BF16), ((all_rows, 3 * hidden), BF16), ((all_rows, half + 3 * hidden), BF16)],
        "expert",
        (*zs, *held),
        2 * all_rows * features * hidden * 5,
        6 * features * hidden,
        10 + 6 * groups,
    )
    back = [messages[0]] + [swap_by(messages[j], j) for j in range(1, SPLIT)]
    send, first = lax.optimization_barrier((send, back[-1]))
    back[-1] = first
    peer = lax.ppermute(send, "dp", [(0, 1), (1, 0)])
    gate_grad, up_grad, down_grad = call(
        weights_kernel,
        [((hidden, half), BF16)] * 3,
        "weights",
        (keep, hid, peer),
        2 * 2 * all_rows * half * hidden * 3,
        6 * half * hidden,
        6 + 2 * groups,
    )
    total = sum(b[MAIN:].astype(F32) for b in back[::-1]).astype(BF16)
    homes = [
        swap_by(total[k * MAIN : (k + 1) * MAIN], SPLIT * (k + 1)) for k in range(window - 1)
    ]
    gate_grad, up_grad, down_grad, *homes = lax.optimization_barrier(
        (gate_grad, up_grad, down_grad, *homes)
    )
    in_grad, combine = call(
        finish_kernel,
        [((toks, features), BF16), ((choices.shape[1], toks), F32)],
        "finish",
        (picks, ranks, *back, *homes),
        2 * toks * features * 16 * (SPLIT + window),
        2 * toks * features,
        6 + window,
        scratch=[pltpu.VMEM((toks, features), BF16), pltpu.SemaphoreType.DMA((MAIN // 2,))],
        out_specs=[HBM, VM],
    )
    return (
        in_grad,
        combine.T,
        gate_grad.T[None],
        up_grad.T[None],
        down_grad[None],
    )


def solution(mesh):
    return jax.shard_map(
        body,
        mesh=mesh,
        in_specs=(
            P(("groups", "expert", "dp"), None),
            P(("groups", "expert", "dp"), None),
            P(("groups", "expert", "dp"), None),
            P(("groups", "expert", "dp"), None),
            P("expert", None, None),
            P("expert", None, None),
            P("expert", None, None),
        ),
        out_specs=(
            P(("groups", "expert", "dp"), None),
            P(("groups", "expert", "dp"), None),
            P(("groups", "expert"), "dp", None),
            P(("groups", "expert"), "dp", None),
            P(("groups", "expert"), None, "dp"),
        ),
        check_vma=False,
    )
```

```python
import jax
import jax.numpy as jnp
from jax import lax
from jax.experimental import pallas as pl
from jax.experimental.pallas import tpu as pltpu
from jax.sharding import PartitionSpec as P

SPLIT = 4
MAIN = 8
TILE = 128
GROUP = 8
MIB = 1024 * 1024
VMEM_LIMIT = 60 * MIB
F32 = jnp.float32
BF16 = jnp.bfloat16


def iota(shape, axis):
    return lax.broadcasted_iota(jnp.int32, shape, axis)


def dot(a, b, contract):
    return lax.dot_general(a, b, ((contract[:1], contract[1:]), ((), ())), preferred_element_type=F32)


def places(picks, expert):
    named = [jnp.any(picks == e, axis=0, keepdims=True) for e in expert]
    table = jnp.concatenate([n.astype(F32) for n in named], axis=0)
    count, toks = table.shape
    pad = -count % 8
    if pad:
        table = jnp.concatenate([table, jnp.zeros((pad, toks), F32)], axis=0)
    before = (iota((toks, toks), 0) < iota((toks, toks), 1)).astype(BF16)
    rank = dot(table.astype(BF16), before, (1, 0))
    return jnp.where(table > 0, rank, -1.0)


def pack_kernel(picks_hbm, gates_hbm, tok_hbm, grad_hbm, *refs):
    outs, rank_ref = refs[:-6], refs[-6]
    picks_ref, gates_ref, tok_ref, grad_ref, sems = refs[-5:]
    loads = [
        pltpu.make_async_copy(src, dst, sems.at[i])
        for i, (src, dst) in enumerate(
            [(picks_hbm, picks_ref), (gates_hbm, gates_ref), (tok_hbm, tok_ref), (grad_hbm, grad_ref)]
        )
    ]
    for load in loads:
        load.start()
    window = len(outs)
    loads[0].wait()
    loads[1].wait()
    quad = lax.axis_index("expert") // SPLIT
    picks = picks_ref[...]
    gates = gates_ref[...].astype(F32)
    features = tok_ref.shape[1]
    fold = features // MAIN
    experts = [quad ^ k for k in range(window)]
    table = places(picks, experts)
    rank_ref[...] = table
    ranks = [table[k : k + 1] for k in range(window)]
    toks = picks.shape[1]
    seat = iota((MAIN, toks), 0).astype(F32)
    mains = [(r == seat).astype(F32) for r in ranks]
    last = jnp.concatenate([(r == float(MAIN)).astype(F32) for r in ranks], axis=0)
    pad = -window % 8
    if pad:
        last = jnp.concatenate([last, jnp.zeros((pad, toks), F32)], axis=0)
    choose = jnp.concatenate(mains + [last], axis=0).astype(BF16)
    loads[2].wait()
    tok_rows = dot(choose, tok_ref[...], (1, 0))
    loads[3].wait()
    grad_rows = dot(choose, grad_ref[...], (1, 0))
    row = iota((MAIN, fold), 0)
    lane = iota((MAIN, TILE), 1)
    for k, out in enumerate(outs):
        top = slice(k * MAIN, (k + 1) * MAIN)
        out[:, :features] = jnp.concatenate([tok_rows[top], grad_rows[top]], axis=0).astype(BF16)
        folded = []
        for rows in (tok_rows, grad_rows):
            at = window * MAIN + k
            total = jnp.zeros((MAIN, fold), F32)
            for c in range(MAIN):
                total = jnp.where(row == c, rows[at : at + 1, c * fold : (c + 1) * fold], total)
            folded.append(total)
        out[:, features : features + fold] = jnp.concatenate(folded, axis=0).astype(BF16)
        weight = jnp.sum(jnp.where(picks == experts[k], gates, 0.0), axis=0, keepdims=True)
        seat_gate = jnp.sum(mains[k] * weight, axis=1, keepdims=True)
        last_gate = jnp.sum(last[k : k + 1] * weight, axis=1, keepdims=True)
        tile = jnp.where(lane == 0, seat_gate, jnp.where(lane == 1, last_gate, 0.0))
        out[:, features + fold :] = jnp.concatenate([tile, tile], axis=0).astype(BF16)


def fetch_kernel(gate_hbm, up_hbm, down_hbm, *refs):
    gate_ref, up_ref, across_ref, down_ref, sems = refs[-5:]
    held = (gate_ref, up_ref, down_ref)
    loads = [
        pltpu.make_async_copy(src, dst, sems.at[i])
        for i, (src, dst) in enumerate(zip((gate_hbm, up_hbm, down_hbm), held))
    ]
    for load in loads:
        load.start()
    hidden = gate_ref.shape[0]
    for i, (load, ref) in enumerate(zip(loads, held)):
        load.wait()
        across_ref[:, i * hidden : (i + 1) * hidden] = ref[...].T


def expert_kernel(*refs):
    wg_ref, wu_ref, across_ref, m0, m1, m2, m3, keep_ref, hid_ref, send_ref = refs[-10:]
    zs, ms = refs[:-10], (m0, m1, m2, m3)
    features = wg_ref.shape[1]
    hidden = wg_ref.shape[0]
    fold = features // MAIN
    half = features // 2
    core = lax.axis_index("dp")
    pair = 2 * MAIN
    per = GROUP // SPLIT
    held = GROUP // len(zs)
    rows_in = held * pair
    groups = zs[0].shape[0] // rows_in

    def work(g):
        if groups == 1:
            src = slice(0, rows_in)
            dst = slice(0, per * MAIN)
            all_rows = slice(0, (GROUP + 1) * pair)
        else:
            src = pl.ds(pl.multiple_of(g * rows_in, rows_in), rows_in)
            dst = pl.ds(pl.multiple_of(g * per * MAIN, per * MAIN), per * MAIN)
            all_rows = pl.ds(pl.multiple_of(g * (GROUP + 1) * pair, pair), (GROUP + 1) * pair)
        main = [z[src, :features] for z in zs]
        bent = jnp.concatenate([z[src, features : features + fold] for z in zs], axis=0)
        tiles = [z[src, features + fold :].astype(F32) for z in zs]
        n = GROUP * pair
        r, q = iota((n, n), 0), iota((n, n), 1)
        swap = ((r & 8) == (q & 8)) & ((r >> 4) == (q & 7)) & ((r & 7) == (q >> 4))
        flat = dot(swap.astype(BF16), bent, (1, 0)).astype(BF16)
        ninth = jnp.concatenate([flat[c * pair : (c + 1) * pair] for c in range(MAIN)], axis=1)
        rows = jnp.concatenate(main + [ninth], axis=0)
        pre = dot(rows, across_ref[...], (1, 0))
        pre_gate, pre_up, back = (pre[:, i * hidden : (i + 1) * hidden] for i in range(3))
        pieces = GROUP + 1
        upper = lambda v: v.reshape(pieces, 2, MAIN, hidden)[:, 0].reshape(pieces * MAIN, hidden)
        lower = lambda v: v.reshape(pieces, 2, MAIN, hidden)[:, 1].reshape(pieces * MAIN, hidden)
        pre_gate, pre_up, back = upper(pre_gate), upper(pre_up), lower(back)
        columns = []
        last = jnp.zeros((MAIN, 1), F32)
        seat = iota((MAIN, 1), 0)
        for p in range(GROUP):
            tile = tiles[p // held][(p % held) * pair : (p % held) * pair + MAIN]
            columns.append(tile[:, 0:1])
            last = jnp.where(seat == p, tile[:, 1:2], last)
        gate = jnp.concatenate(columns + [last], axis=0)
        sig = 1.0 / (1.0 + jnp.exp(-pre_gate))
        silu = pre_gate * sig
        slope = sig * (1.0 + pre_gate * (1.0 - sig))
        act = silu * pre_up
        combine = jnp.sum(back * act, axis=1, keepdims=True)
        scaled = gate * act
        gated = gate * back
        g_gate = (gated * slope * pre_up).astype(BF16)
        g_up = (gated * silu).astype(BF16)
        part = dot(g_gate, wg_ref[...], (1, 0)) + dot(g_up, wu_ref[...], (1, 0))
        tail = part[GROUP * MAIN :].astype(BF16).astype(F32)
        stack = jnp.concatenate([tail[:, c * fold : (c + 1) * fold] for c in range(MAIN)], axis=0)
        n = GROUP * MAIN
        r, q = iota((n, n), 0), iota((n, n), 1)
        turn = ((r >> 3) == (q & 7)) & ((r & 7) == (q >> 3))
        folded = dot(turn.astype(BF16), stack.astype(BF16), (1, 0))
        lane = iota((MAIN, TILE), 1)
        notes = []
        for p in range(GROUP):
            at = GROUP * MAIN + p
            notes.append(
                jnp.where(
                    lane == 0,
                    combine[p * MAIN : (p + 1) * MAIN],
                    jnp.where(lane == 1, combine[at : at + 1], 0.0),
                )
            )
        for j, m in enumerate(ms):
            span = slice(j * per * MAIN, (j + 1) * per * MAIN)
            m[dst, :features] = part[span].astype(BF16)
            m[dst, features : features + fold] = folded[span].astype(BF16)
            m[dst, features + fold :] = jnp.concatenate(
                notes[j * per : (j + 1) * per], axis=0
            ).astype(BF16)
        none = jnp.zeros((pieces, MAIN, hidden), F32)

        def lay(v, place):
            v = v.astype(F32).reshape(pieces, MAIN, hidden)
            both = [v, none] if place == 0 else [none, v]
            return jnp.stack(both, axis=1).reshape(pieces * 2 * MAIN, hidden).astype(BF16)

        hid = [lay(g_gate, 0), lay(g_up, 0), lay(scaled, 1)]
        low, high = rows[:, :half], rows[:, half:]
        keep_ref[all_rows, :] = jnp.where(core == 0, low, high)
        send_ref[all_rows, :half] = jnp.where(core == 0, high, low)
        for i, h in enumerate(hid):
            hid_ref[all_rows, i * hidden : (i + 1) * hidden] = h
            send_ref[all_rows, half + i * hidden : half + (i + 1) * hidden] = h

    if groups == 1:
        work(0)
    else:
        lax.fori_loop(0, groups, lambda g, c: (work(g), c)[1], 0)


def weights_kernel(keep_ref, hid_ref, peer_ref, gate_ref, up_ref, down_ref):
    half = keep_ref.shape[1]
    hidden = gate_ref.shape[0]
    outs = (gate_ref, up_ref, down_ref)
    for i, out in enumerate(outs):
        cols = slice(i * hidden, (i + 1) * hidden)
        far = slice(half + i * hidden, half + (i + 1) * hidden)
        total = dot(hid_ref[:, cols], keep_ref[...], (0, 0))
        total = total + dot(peer_ref[:, far], peer_ref[:, :half], (0, 0))
        out[...] = total.astype(BF16)


def finish_kernel(picks_ref, rank_ref, o0, o1, o2, o3, *rest):
    far, (grad_ref, comb_ref) = rest[:-2], rest[-2:]
    window = 1 + len(far)
    quad = lax.axis_index("expert") // SPLIT
    picks = picks_ref[...]
    experts = [quad ^ k for k in range(window)]
    ranks = [rank_ref[k : k + 1, :] for k in range(window)]
    features = grad_ref.shape[1]
    fold = features // MAIN
    toks = picks.shape[1]
    seat = iota((MAIN, toks), 0).astype(F32)
    mains = [(r == seat).astype(F32) for r in ranks]
    lasts = [(r == float(MAIN)).astype(F32) for r in ranks]
    blocks = [(0, o[:MAIN, :].astype(F32)) for o in (o0, o1, o2, o3)]
    blocks += [(1 + k, f[...].astype(F32)) for k, f in enumerate(far)]
    row = iota((MAIN, toks), 0)
    for c in range(MAIN):
        cols = slice(c * fold, (c + 1) * fold)
        left, right = [], []
        for k, v in blocks:
            left += [mains[k], jnp.where(row == c, lasts[k], 0.0)]
            right += [v[:, cols], v[:, features : features + fold]]
        left = jnp.concatenate(left, axis=0).astype(BF16)
        right = jnp.concatenate(right, axis=0).astype(BF16)
        grad_ref[:, cols] = dot(left, right, (0, 0)).astype(BF16)
    terms = [jnp.zeros((1, toks), F32) for _ in range(window)]
    for k, v in blocks:
        note = v[:, features + fold :]
        terms[k] = terms[k] + jnp.sum(mains[k] * note[:, 0:1], axis=0, keepdims=True)
        terms[k] = terms[k] + lasts[k] * note[0:1, 1:2]
    comb = jnp.zeros(picks.shape, F32)
    for k in range(window):
        comb = comb + jnp.where(picks == experts[k], terms[k], 0.0)
    comb_ref[...] = comb


VM = pl.BlockSpec(memory_space=pltpu.VMEM)
HBM = pl.BlockSpec(memory_space=pltpu.HBM)
ANY = pl.BlockSpec(memory_space=pl.ANY)


def call(kernel, outs, name, args, flops, nbytes, room, specs=None, scratch=()):
    specs = specs or [VM] * len(args)
    args = [
        pltpu.with_memory_space_constraint(a, pltpu.HBM) if s is HBM else a
        for a, s in zip(args, specs)
    ]
    return pl.pallas_call(
        kernel,
        out_shape=[jax.ShapeDtypeStruct(s, t) for s, t in outs],
        in_specs=specs,
        out_specs=[VM] * len(outs),
        scratch_shapes=list(scratch),
        compiler_params=pltpu.CompilerParams(vmem_limit_bytes=min(VMEM_LIMIT, room * MIB)),
        cost_estimate=pl.CostEstimate(flops=flops, bytes_accessed=nbytes, transcendentals=0),
        name=name,
    )(*args)


def swap_by(block, mask):
    count = lax.axis_size("expert")
    return lax.ppermute(block, "expert", [(i, i ^ mask) for i in range(count)])


def body(tokens, out_grad, choices, gates, gate_weight, up_weight, down_weight):
    members = lax.axis_size("expert")
    toks, features = tokens.shape
    hidden = gate_weight.shape[2]
    window = members // SPLIT
    fold = features // MAIN
    half = features // 2
    width = features + fold + TILE
    picks, gates_t = choices.T, gates.T
    wg, wu, wd = gate_weight[0].T, up_weight[0].T, down_weight[0]
    groups = members // GROUP

    *packed, ranks = call(
        pack_kernel,
        [((2 * MAIN, width), BF16)] * window + [((-(-window // 8) * 8, toks), F32)],
        "pack",
        (picks, gates_t, tokens, out_grad),
        2 * (MAIN + 1) * window * toks * features * 2,
        4 * toks * features,
        6 + window,
        [HBM] * 4,
        [pltpu.VMEM(v.shape, v.dtype) for v in (picks, gates_t, tokens, out_grad)]
        + [pltpu.SemaphoreType.DMA((4,))],
    )
    own, others = packed[0], packed[1:]
    arrived = [swap_by(o, SPLIT * (k + 1)) for k, o in enumerate(others)]
    near = [own] + [swap_by(own, j) for j in range(1, SPLIT)]
    held = call(
        fetch_kernel,
        [(wg.shape, BF16), (wu.shape, BF16), ((features, 3 * hidden), BF16)],
        "fetch",
        (wg, wu, wd, *near[1:]),
        0,
        6 * features * hidden,
        12,
        [HBM] * 3 + [ANY] * (SPLIT - 1),
        [pltpu.VMEM(wd.shape, BF16), pltpu.SemaphoreType.DMA((3,))],
    )
    from_far = arrived[0] if window == 2 else jnp.concatenate(arrived, axis=0)
    far = [from_far] + [swap_by(from_far, j) for j in range(1, SPLIT)]
    pairs = list(zip(near, far))
    if groups == 1:
        zs = [z for pair in pairs for z in pair]
    else:
        zs = [jnp.concatenate(pair, axis=0) for pair in pairs]

    all_rows = groups * (GROUP + 1) * 2 * MAIN
    *messages, keep, hid, send = call(
        expert_kernel,
        [((window * MAIN, width), BF16)] * SPLIT
        + [((all_rows, half), BF16), ((all_rows, 3 * hidden), BF16), ((all_rows, half + 3 * hidden), BF16)],
        "expert",
        (*zs, *held),
        2 * all_rows * features * hidden * 5,
        6 * features * hidden,
        10 + 6 * groups,
    )
    back = [messages[0]] + [swap_by(messages[j], j) for j in range(1, SPLIT)]
    send, first = lax.optimization_barrier((send, back[-1]))
    back[-1] = first
    peer = lax.ppermute(send, "dp", [(0, 1), (1, 0)])
    gate_grad, up_grad, down_grad = call(
        weights_kernel,
        [((hidden, half), BF16)] * 3,
        "weights",
        (keep, hid, peer),
        2 * 2 * all_rows * half * hidden * 3,
        6 * half * hidden,
        6 + 2 * groups,
    )
    total = sum(b[MAIN:].astype(F32) for b in back[::-1]).astype(BF16)
    homes = [
        swap_by(total[k * MAIN : (k + 1) * MAIN], SPLIT * (k + 1)) for k in range(window - 1)
    ]
    gate_grad, up_grad, down_grad, *homes = lax.optimization_barrier(
        (gate_grad, up_grad, down_grad, *homes)
    )
    in_grad, combine = call(
        finish_kernel,
        [((toks, features), BF16), ((choices.shape[1], toks), F32)],
        "finish",
        (picks, ranks, *back, *homes),
        2 * toks * features * 16 * (SPLIT + window),
        2 * toks * features,
        6 + window,
    )
    return (
        in_grad,
        combine.T,
        gate_grad.T[None],
        up_grad.T[None],
        down_grad[None],
    )


def solution(mesh):
    return jax.shard_map(
        body,
        mesh=mesh,
        in_specs=(
            P(("groups", "expert", "dp"), None),
            P(("groups", "expert", "dp"), None),
            P(("groups", "expert", "dp"), None),
            P(("groups", "expert", "dp"), None),
            P("expert", None, None),
            P("expert", None, None),
            P("expert", None, None),
        ),
        out_specs=(
            P(("groups", "expert", "dp"), None),
            P(("groups", "expert", "dp"), None),
            P(("groups", "expert"), "dp", None),
            P(("groups", "expert"), "dp", None),
            P(("groups", "expert"), None, "dp"),
        ),
        check_vma=False,
    )
```

```python
import jax
import jax.numpy as jnp
from jax import lax
from jax.experimental import pallas as pl
from jax.experimental.pallas import tpu as pltpu
from jax.sharding import PartitionSpec as P

SPLIT = 4
MAIN = 8
TILE = 128
PIECES = 4
GROUP = 8
MIB = 1024 * 1024
VMEM_LIMIT = 60 * MIB
F32 = jnp.float32
BF16 = jnp.bfloat16


def iota(shape, axis):
    return lax.broadcasted_iota(jnp.int32, shape, axis)


def dot(a, b, contract):
    return lax.dot_general(a, b, ((contract[:1], contract[1:]), ((), ())), preferred_element_type=F32)


def places(picks, expert):
    named = [jnp.any(picks == e, axis=0, keepdims=True) for e in expert]
    table = jnp.concatenate([n.astype(F32) for n in named], axis=0)
    count, toks = table.shape
    pad = -count % 8
    if pad:
        table = jnp.concatenate([table, jnp.zeros((pad, toks), F32)], axis=0)
    before = (iota((toks, toks), 0) < iota((toks, toks), 1)).astype(BF16)
    rank = dot(table.astype(BF16), before, (1, 0))
    return jnp.where(table > 0, rank, -1.0)


def pack_kernel(picks_hbm, gates_hbm, tok_hbm, grad_hbm, *refs):
    outs, rank_ref = refs[:-6], refs[-6]
    picks_ref, gates_ref, tok_ref, grad_ref, sems = refs[-5:]
    moves = [
        (picks_hbm, picks_ref), (gates_hbm, gates_ref), (tok_hbm, tok_ref), (grad_hbm, grad_ref)
    ]
    loads = [pltpu.make_async_copy(src, dst, sems.at[i]) for i, (src, dst) in enumerate(moves)]
    for load in loads:
        load.start()
    window = len(outs)
    for load in loads[:2]:
        load.wait()
    quad = lax.axis_index("expert") // SPLIT
    picks = picks_ref[...]
    gates = gates_ref[...].astype(F32)
    features = tok_ref.shape[1]
    fold = features // MAIN
    experts = [quad ^ k for k in range(window)]
    table = places(picks, experts)
    rank_ref[...] = table
    ranks = [table[k : k + 1] for k in range(window)]
    toks = picks.shape[1]
    seat = iota((MAIN, toks), 0).astype(F32)
    mains = [(r == seat).astype(F32) for r in ranks]
    last = jnp.concatenate([(r == float(MAIN)).astype(F32) for r in ranks], axis=0)
    pad = -window % 8
    if pad:
        last = jnp.concatenate([last, jnp.zeros((pad, toks), F32)], axis=0)
    choose = jnp.concatenate(mains + [last], axis=0).astype(BF16)
    loads[2].wait()
    tok_rows = dot(choose, tok_ref[...], (1, 0))
    loads[3].wait()
    grad_rows = dot(choose, grad_ref[...], (1, 0))
    row = iota((MAIN, fold), 0)
    lane = iota((MAIN, TILE), 1)
    for k, out in enumerate(outs):
        top = slice(k * MAIN, (k + 1) * MAIN)
        out[:, :features] = jnp.concatenate([tok_rows[top], grad_rows[top]], axis=0).astype(BF16)
        folded = []
        for rows in (tok_rows, grad_rows):
            at = window * MAIN + k
            total = jnp.zeros((MAIN, fold), F32)
            for c in range(MAIN):
                total = jnp.where(row == c, rows[at : at + 1, c * fold : (c + 1) * fold], total)
            folded.append(total)
        out[:, features : features + fold] = jnp.concatenate(folded, axis=0).astype(BF16)
        weight = jnp.sum(jnp.where(picks == experts[k], gates, 0.0), axis=0, keepdims=True)
        seat_gate = jnp.sum(mains[k] * weight, axis=1, keepdims=True)
        last_gate = jnp.sum(last[k : k + 1] * weight, axis=1, keepdims=True)
        tile = jnp.where(lane == 0, seat_gate, jnp.where(lane == 1, last_gate, 0.0))
        out[:, features + fold :] = jnp.concatenate([tile, tile], axis=0).astype(BF16)


def fetch_kernel(gate_hbm, up_hbm, down_hbm, *refs):
    gate_ref, up_ref, across_ref, down_ref, sems = refs[-5:]
    held = (gate_ref, up_ref, down_ref)
    loads = [
        pltpu.make_async_copy(src, dst, sems.at[i])
        for i, (src, dst) in enumerate(zip((gate_hbm, up_hbm, down_hbm), held))
    ]
    for load in loads:
        load.start()
    hidden = gate_ref.shape[0]
    for i, (load, ref) in enumerate(zip(loads, held)):
        load.wait()
        across_ref[:, i * hidden : (i + 1) * hidden] = ref[...].T


def expert_kernel(*refs):
    wg_ref, wu_ref, across_ref, m0, m1, m2, m3, keep_ref, hid_ref, send_ref = refs[-10:]
    zs, ms = refs[:-10], (m0, m1, m2, m3)
    features = wg_ref.shape[1]
    hidden = wg_ref.shape[0]
    fold = features // MAIN
    half = features // 2
    core = lax.axis_index("dp")
    pair = 2 * MAIN
    per = GROUP // SPLIT
    held = GROUP // len(zs)
    rows_in = held * pair
    groups = zs[0].shape[0] // rows_in

    def work(g):
        if groups == 1:
            src = slice(0, rows_in)
            dst = slice(0, per * MAIN)
            all_rows = slice(0, (GROUP + 1) * pair)
        else:
            src = pl.ds(pl.multiple_of(g * rows_in, rows_in), rows_in)
            dst = pl.ds(pl.multiple_of(g * per * MAIN, per * MAIN), per * MAIN)
            all_rows = pl.ds(pl.multiple_of(g * (GROUP + 1) * pair, pair), (GROUP + 1) * pair)
        main = [z[src, :features] for z in zs]
        bent = jnp.concatenate([z[src, features : features + fold] for z in zs], axis=0)
        tiles = [z[src, features + fold :].astype(F32) for z in zs]
        n = GROUP * pair
        r, q = iota((n, n), 0), iota((n, n), 1)
        swap = ((r & 8) == (q & 8)) & ((r >> 4) == (q & 7)) & ((r & 7) == (q >> 4))
        flat = dot(swap.astype(BF16), bent, (1, 0)).astype(BF16)
        ninth = jnp.concatenate([flat[c * pair : (c + 1) * pair] for c in range(MAIN)], axis=1)
        rows = jnp.concatenate(main + [ninth], axis=0)
        pre = dot(rows, across_ref[...], (1, 0))
        pre_gate, pre_up, back = (pre[:, i * hidden : (i + 1) * hidden] for i in range(3))
        pieces = GROUP + 1
        upper = lambda v: v.reshape(pieces, 2, MAIN, hidden)[:, 0].reshape(pieces * MAIN, hidden)
        lower = lambda v: v.reshape(pieces, 2, MAIN, hidden)[:, 1].reshape(pieces * MAIN, hidden)
        pre_gate, pre_up, back = upper(pre_gate), upper(pre_up), lower(back)
        columns = []
        last = jnp.zeros((MAIN, 1), F32)
        seat = iota((MAIN, 1), 0)
        for p in range(GROUP):
            tile = tiles[p // held][(p % held) * pair : (p % held) * pair + MAIN]
            columns.append(tile[:, 0:1])
            last = jnp.where(seat == p, tile[:, 1:2], last)
        gate = jnp.concatenate(columns + [last], axis=0)
        sig = 1.0 / (1.0 + jnp.exp(-pre_gate))
        silu = pre_gate * sig
        slope = sig * (1.0 + pre_gate * (1.0 - sig))
        act = silu * pre_up
        combine = jnp.sum(back * act, axis=1, keepdims=True)
        scaled = gate * act
        gated = gate * back
        g_gate = (gated * slope * pre_up).astype(BF16)
        g_up = (gated * silu).astype(BF16)
        part = dot(g_gate, wg_ref[...], (1, 0)) + dot(g_up, wu_ref[...], (1, 0))
        tail = part[GROUP * MAIN :].astype(BF16).astype(F32)
        stack = jnp.concatenate([tail[:, c * fold : (c + 1) * fold] for c in range(MAIN)], axis=0)
        n = GROUP * MAIN
        r, q = iota((n, n), 0), iota((n, n), 1)
        turn = ((r >> 3) == (q & 7)) & ((r & 7) == (q >> 3))
        folded = dot(turn.astype(BF16), stack.astype(BF16), (1, 0))
        lane = iota((MAIN, TILE), 1)
        notes = []
        for p in range(GROUP):
            at = GROUP * MAIN + p
            notes.append(
                jnp.where(
                    lane == 0,
                    combine[p * MAIN : (p + 1) * MAIN],
                    jnp.where(lane == 1, combine[at : at + 1], 0.0),
                )
            )
        for j, m in enumerate(ms):
            span = slice(j * per * MAIN, (j + 1) * per * MAIN)
            m[dst, :features] = part[span].astype(BF16)
            m[dst, features : features + fold] = folded[span].astype(BF16)
            m[dst, features + fold :] = jnp.concatenate(
                notes[j * per : (j + 1) * per], axis=0
            ).astype(BF16)
        none = jnp.zeros((pieces, MAIN, hidden), F32)

        def lay(v, place):
            v = v.astype(F32).reshape(pieces, MAIN, hidden)
            both = [v, none] if place == 0 else [none, v]
            return jnp.stack(both, axis=1).reshape(pieces * 2 * MAIN, hidden).astype(BF16)

        hid = [lay(g_gate, 0), lay(g_up, 0), lay(scaled, 1)]
        low, high = rows[:, :half], rows[:, half:]
        keep_ref[all_rows, :] = jnp.where(core == 0, low, high)
        send_ref[all_rows, :half] = jnp.where(core == 0, high, low)
        for i, h in enumerate(hid):
            hid_ref[all_rows, i * hidden : (i + 1) * hidden] = h
            send_ref[all_rows, half + i * hidden : half + (i + 1) * hidden] = h

    if groups == 1:
        work(0)
    else:
        lax.fori_loop(0, groups, lambda g, c: (work(g), c)[1], 0)


def weights_kernel(keep_ref, hid_ref, peer_ref, gate_ref, up_ref, down_ref):
    half = keep_ref.shape[1]
    hidden = gate_ref.shape[0]
    outs = (gate_ref, up_ref, down_ref)
    for i, out in enumerate(outs):
        cols = slice(i * hidden, (i + 1) * hidden)
        far = slice(half + i * hidden, half + (i + 1) * hidden)
        total = dot(hid_ref[:, cols], keep_ref[...], (0, 0))
        total = total + dot(peer_ref[:, far], peer_ref[:, :half], (0, 0))
        out[...] = total.astype(BF16)


def finish_kernel(picks_ref, rank_ref, o0, o1, o2, o3, *rest):
    far, (grad_hbm, comb_hbm, grad_ref, comb_ref, sems) = rest[:-5], rest[-5:]
    window = 1 + len(far)
    quad = lax.axis_index("expert") // SPLIT
    picks = picks_ref[...]
    experts = [quad ^ k for k in range(window)]
    ranks = [rank_ref[k : k + 1, :] for k in range(window)]
    features = grad_ref.shape[1]
    fold = features // MAIN
    toks = picks.shape[1]
    seat = iota((MAIN, toks), 0).astype(F32)
    mains = [(r == seat).astype(F32) for r in ranks]
    lasts = [(r == float(MAIN)).astype(F32) for r in ranks]
    blocks = [(0, o[:MAIN, :].astype(F32)) for o in (o0, o1, o2, o3)]
    blocks += [(1 + k, f[...].astype(F32)) for k, f in enumerate(far)]
    terms = [jnp.zeros((1, toks), F32) for _ in range(window)]
    for k, v in blocks:
        note = v[:, features + fold :]
        terms[k] = terms[k] + jnp.sum(mains[k] * note[:, 0:1], axis=0, keepdims=True)
        terms[k] = terms[k] + lasts[k] * note[0:1, 1:2]
    comb = jnp.zeros(picks.shape, F32)
    for k in range(window):
        comb = comb + jnp.where(picks == experts[k], terms[k], 0.0)
    comb_ref[...] = comb
    stores = [pltpu.make_async_copy(comb_ref, comb_hbm, sems.at[PIECES])]
    stores[0].start()
    row = iota((MAIN, toks), 0)
    each = MAIN // PIECES
    for c in range(MAIN):
        cols = slice(c * fold, (c + 1) * fold)
        left, right = [], []
        for k, v in blocks:
            left += [mains[k], jnp.where(row == c, lasts[k], 0.0)]
            right += [v[:, cols], v[:, features : features + fold]]
        left = jnp.concatenate(left, axis=0).astype(BF16)
        right = jnp.concatenate(right, axis=0).astype(BF16)
        grad_ref[:, cols] = dot(left, right, (0, 0)).astype(BF16)
        if c % each == each - 1:
            done = slice((c + 1 - each) * fold, (c + 1) * fold)
            store = pltpu.make_async_copy(
                grad_ref.at[:, done], grad_hbm.at[:, done], sems.at[c // each]
            )
            store.start()
            stores.append(store)
    for store in stores:
        store.wait()


VM = pl.BlockSpec(memory_space=pltpu.VMEM)
HBM = pl.BlockSpec(memory_space=pltpu.HBM)
ANY = pl.BlockSpec(memory_space=pl.ANY)


def call(kernel, outs, name, args, flops, nbytes, room, specs=None, scratch=(), out_specs=None):
    specs = specs or [VM] * len(args)
    args = [
        pltpu.with_memory_space_constraint(a, pltpu.HBM) if s is HBM else a
        for a, s in zip(args, specs)
    ]
    return pl.pallas_call(
        kernel,
        out_shape=[jax.ShapeDtypeStruct(s, t) for s, t in outs],
        in_specs=specs,
        out_specs=out_specs or [VM] * len(outs),
        scratch_shapes=list(scratch),
        compiler_params=pltpu.CompilerParams(vmem_limit_bytes=min(VMEM_LIMIT, room * MIB)),
        cost_estimate=pl.CostEstimate(flops=flops, bytes_accessed=nbytes, transcendentals=0),
        name=name,
    )(*args)


def swap_by(block, mask):
    count = lax.axis_size("expert")
    return lax.ppermute(block, "expert", [(i, i ^ mask) for i in range(count)])


def body(tokens, out_grad, choices, gates, gate_weight, up_weight, down_weight):
    members = lax.axis_size("expert")
    toks, features = tokens.shape
    hidden = gate_weight.shape[2]
    window = members // SPLIT
    fold = features // MAIN
    half = features // 2
    width = features + fold + TILE
    picks, gates_t = choices.T, gates.T
    wg, wu, wd = gate_weight[0].T, up_weight[0].T, down_weight[0]
    groups = members // GROUP

    *packed, ranks = call(
        pack_kernel,
        [((2 * MAIN, width), BF16)] * window + [((-(-window // 8) * 8, toks), F32)],
        "pack",
        (picks, gates_t, tokens, out_grad),
        2 * (MAIN + 1) * window * toks * features * 2,
        4 * toks * features,
        6 + window,
        [HBM] * 4,
        [pltpu.VMEM(v.shape, v.dtype) for v in (picks, gates_t, tokens, out_grad)]
        + [pltpu.SemaphoreType.DMA((4,))],
    )
    own, others = packed[0], packed[1:]
    arrived = [swap_by(o, SPLIT * (k + 1)) for k, o in enumerate(others)]
    near = [own] + [swap_by(own, j) for j in range(1, SPLIT)]
    held = call(
        fetch_kernel,
        [(wg.shape, BF16), (wu.shape, BF16), ((features, 3 * hidden), BF16)],
        "fetch",
        (wg, wu, wd, near[-1]),
        0,
        6 * features * hidden,
        12,
        [HBM] * 3 + [ANY],
        [pltpu.VMEM(wd.shape, BF16), pltpu.SemaphoreType.DMA((3,))],
    )
    from_far = arrived[0] if window == 2 else jnp.concatenate(arrived, axis=0)
    far = [from_far] + [swap_by(from_far, j) for j in range(1, SPLIT)]
    pairs = list(zip(near, far))
    if groups == 1:
        zs = [z for pair in pairs for z in pair]
    else:
        zs = [jnp.concatenate(pair, axis=0) for pair in pairs]

    all_rows = groups * (GROUP + 1) * 2 * MAIN
    *messages, keep, hid, send = call(
        expert_kernel,
        [((window * MAIN, width), BF16)] * SPLIT
        + [((all_rows, half), BF16), ((all_rows, 3 * hidden), BF16), ((all_rows, half + 3 * hidden), BF16)],
        "expert",
        (*zs, *held),
        2 * all_rows * features * hidden * 5,
        6 * features * hidden,
        10 + 6 * groups,
    )
    back = [messages[0]] + [swap_by(messages[j], j) for j in range(1, SPLIT)]
    send, first = lax.optimization_barrier((send, back[-1]))
    back[-1] = first
    peer = lax.ppermute(send, "dp", [(0, 1), (1, 0)])
    gate_grad, up_grad, down_grad = call(
        weights_kernel,
        [((hidden, half), BF16)] * 3,
        "weights",
        (keep, hid, peer),
        2 * 2 * all_rows * half * hidden * 3,
        6 * half * hidden,
        6 + 2 * groups,
    )
    total = sum(b[MAIN:].astype(F32) for b in back[::-1]).astype(BF16)
    homes = [
        swap_by(total[k * MAIN : (k + 1) * MAIN], SPLIT * (k + 1)) for k in range(window - 1)
    ]
    gate_grad, up_grad, down_grad, *homes = lax.optimization_barrier(
        (gate_grad, up_grad, down_grad, *homes)
    )
    in_grad, combine = call(
        finish_kernel,
        [((toks, features), BF16), ((choices.shape[1], toks), F32)],
        "finish",
        (picks, ranks, *back, *homes),
        2 * toks * features * 16 * (SPLIT + window),
        2 * toks * features,
        6 + window,
        scratch=[
            pltpu.VMEM((toks, features), BF16),
            pltpu.VMEM((choices.shape[1], toks), F32),
            pltpu.SemaphoreType.DMA((PIECES + 1,)),
        ],
        out_specs=[HBM, HBM],
    )
    return (
        in_grad,
        combine.T,
        gate_grad.T[None],
        up_grad.T[None],
        down_grad[None],
    )


def solution(mesh):
    return jax.shard_map(
        body,
        mesh=mesh,
        in_specs=(
            P(("groups", "expert", "dp"), None),
            P(("groups", "expert", "dp"), None),
            P(("groups", "expert", "dp"), None),
            P(("groups", "expert", "dp"), None),
            P("expert", None, None),
            P("expert", None, None),
            P("expert", None, None),
        ),
        out_specs=(
            P(("groups", "expert", "dp"), None),
            P(("groups", "expert", "dp"), None),
            P(("groups", "expert"), "dp", None),
            P(("groups", "expert"), "dp", None),
            P(("groups", "expert"), None, "dp"),
        ),
        check_vma=False,
    )
```

```python
import functools

import jax
import jax.numpy as jnp
from jax import lax
from jax.experimental import pallas as pl
from jax.experimental.pallas import tpu as pltpu
from jax.sharding import PartitionSpec as P

SPLIT = 4
MAIN = 8
TILE = 128
PIECES = 4
GROUP = 8
MIB = 1024 * 1024
VMEM_LIMIT = 60 * MIB
F32 = jnp.float32
BF16 = jnp.bfloat16


def iota(shape, axis):
    return lax.broadcasted_iota(jnp.int32, shape, axis)


def dot(a, b, contract):
    return lax.dot_general(a, b, ((contract[:1], contract[1:]), ((), ())), preferred_element_type=F32)


def places(picks, expert):
    named = [jnp.any(picks == e, axis=0, keepdims=True) for e in expert]
    table = jnp.concatenate([n.astype(F32) for n in named], axis=0)
    count, toks = table.shape
    pad = -count % 8
    if pad:
        table = jnp.concatenate([table, jnp.zeros((pad, toks), F32)], axis=0)
    before = (iota((toks, toks), 0) < iota((toks, toks), 1)).astype(BF16)
    rank = dot(table.astype(BF16), before, (1, 0))
    return jnp.where(table > 0, rank, -1.0)


def pack_kernel(picks_hbm, gates_hbm, tok_hbm, grad_hbm, *refs):
    outs, rank_ref = refs[:-6], refs[-6]
    picks_ref, gates_ref, tok_ref, grad_ref, sems = refs[-5:]
    moves = [
        (picks_hbm, picks_ref), (gates_hbm, gates_ref), (tok_hbm, tok_ref), (grad_hbm, grad_ref)
    ]
    loads = [pltpu.make_async_copy(src, dst, sems.at[i]) for i, (src, dst) in enumerate(moves)]
    for load in loads:
        load.start()
    window = len(outs)
    for load in loads[:2]:
        load.wait()
    quad = lax.axis_index("expert") // SPLIT
    picks = picks_ref[...]
    gates = gates_ref[...].astype(F32)
    features = tok_ref.shape[1]
    fold = features // MAIN
    experts = [quad ^ k for k in range(window)]
    table = places(picks, experts)
    rank_ref[...] = table
    ranks = [table[k : k + 1] for k in range(window)]
    toks = picks.shape[1]
    seat = iota((MAIN, toks), 0).astype(F32)
    mains = [(r == seat).astype(F32) for r in ranks]
    last = jnp.concatenate([(r == float(MAIN)).astype(F32) for r in ranks], axis=0)
    pad = -window % 8
    if pad:
        last = jnp.concatenate([last, jnp.zeros((pad, toks), F32)], axis=0)
    choose = jnp.concatenate(mains + [last], axis=0).astype(BF16)
    loads[2].wait()
    tok_rows = dot(choose, tok_ref[...], (1, 0))
    loads[3].wait()
    grad_rows = dot(choose, grad_ref[...], (1, 0))
    row = iota((MAIN, fold), 0)
    lane = iota((MAIN, TILE), 1)
    for k, out in enumerate(outs):
        top = slice(k * MAIN, (k + 1) * MAIN)
        out[:, :features] = jnp.concatenate([tok_rows[top], grad_rows[top]], axis=0).astype(BF16)
        folded = []
        for rows in (tok_rows, grad_rows):
            at = window * MAIN + k
            total = jnp.zeros((MAIN, fold), F32)
            for c in range(MAIN):
                total = jnp.where(row == c, rows[at : at + 1, c * fold : (c + 1) * fold], total)
            folded.append(total)
        out[:, features : features + fold] = jnp.concatenate(folded, axis=0).astype(BF16)
        weight = jnp.sum(jnp.where(picks == experts[k], gates, 0.0), axis=0, keepdims=True)
        seat_gate = jnp.sum(mains[k] * weight, axis=1, keepdims=True)
        last_gate = jnp.sum(last[k : k + 1] * weight, axis=1, keepdims=True)
        tile = jnp.where(lane == 0, seat_gate, jnp.where(lane == 1, last_gate, 0.0))
        out[:, features + fold :] = jnp.concatenate([tile, tile], axis=0).astype(BF16)


def fetch_kernel(gate_hbm, up_hbm, down_hbm, *refs):
    gate_ref, up_ref, across_ref, down_ref, sems = refs[-5:]
    held = (gate_ref, up_ref, down_ref)
    loads = [
        pltpu.make_async_copy(src, dst, sems.at[i])
        for i, (src, dst) in enumerate(zip((gate_hbm, up_hbm, down_hbm), held))
    ]
    for load in loads:
        load.start()
    hidden = gate_ref.shape[0]
    for i, (load, ref) in enumerate(zip(loads, held)):
        load.wait()
        across_ref[:, i * hidden : (i + 1) * hidden] = ref[...].T


def expert_kernel(inputs, *refs):
    wg_ref, wu_ref, across_ref = refs[inputs : inputs + 3]
    zs, ms, (keep_ref, hid_ref, send_ref) = refs[:inputs], refs[inputs + 3 : -3], refs[-3:]
    features = wg_ref.shape[1]
    hidden = wg_ref.shape[0]
    fold = features // MAIN
    half = features // 2
    core = lax.axis_index("dp")
    pair = 2 * MAIN
    per = GROUP // SPLIT
    held = GROUP // len(zs)
    rows_in = held * pair
    groups = zs[0].shape[0] // rows_in

    def work(g):
        if groups == 1:
            src = slice(0, rows_in)
            all_rows = slice(0, (GROUP + 1) * pair)
        else:
            src = pl.ds(pl.multiple_of(g * rows_in, rows_in), rows_in)
            dst = pl.ds(pl.multiple_of(g * per * MAIN, per * MAIN), per * MAIN)
            all_rows = pl.ds(pl.multiple_of(g * (GROUP + 1) * pair, pair), (GROUP + 1) * pair)
        main = [z[src, :features] for z in zs]
        bent = jnp.concatenate([z[src, features : features + fold] for z in zs], axis=0)
        tiles = [z[src, features + fold :].astype(F32) for z in zs]
        n = GROUP * pair
        r, q = iota((n, n), 0), iota((n, n), 1)
        swap = ((r & 8) == (q & 8)) & ((r >> 4) == (q & 7)) & ((r & 7) == (q >> 4))
        flat = dot(swap.astype(BF16), bent, (1, 0)).astype(BF16)
        ninth = jnp.concatenate([flat[c * pair : (c + 1) * pair] for c in range(MAIN)], axis=1)
        rows = jnp.concatenate(main + [ninth], axis=0)
        pre = dot(rows, across_ref[...], (1, 0))
        pre_gate, pre_up, back = (pre[:, i * hidden : (i + 1) * hidden] for i in range(3))
        pieces = GROUP + 1
        upper = lambda v: v.reshape(pieces, 2, MAIN, hidden)[:, 0].reshape(pieces * MAIN, hidden)
        lower = lambda v: v.reshape(pieces, 2, MAIN, hidden)[:, 1].reshape(pieces * MAIN, hidden)
        pre_gate, pre_up, back = upper(pre_gate), upper(pre_up), lower(back)
        columns = []
        last = jnp.zeros((MAIN, 1), F32)
        seat = iota((MAIN, 1), 0)
        for p in range(GROUP):
            tile = tiles[p // held][(p % held) * pair : (p % held) * pair + MAIN]
            columns.append(tile[:, 0:1])
            last = jnp.where(seat == p, tile[:, 1:2], last)
        gate = jnp.concatenate(columns + [last], axis=0)
        sig = 1.0 / (1.0 + jnp.exp(-pre_gate))
        silu = pre_gate * sig
        slope = sig * (1.0 + pre_gate * (1.0 - sig))
        act = silu * pre_up
        combine = jnp.sum(back * act, axis=1, keepdims=True)
        scaled = gate * act
        gated = gate * back
        g_gate = (gated * slope * pre_up).astype(BF16)
        g_up = (gated * silu).astype(BF16)
        part = dot(g_gate, wg_ref[...], (1, 0)) + dot(g_up, wu_ref[...], (1, 0))
        tail = part[GROUP * MAIN :].astype(BF16).astype(F32)
        stack = jnp.concatenate([tail[:, c * fold : (c + 1) * fold] for c in range(MAIN)], axis=0)
        n = GROUP * MAIN
        r, q = iota((n, n), 0), iota((n, n), 1)
        turn = ((r >> 3) == (q & 7)) & ((r & 7) == (q >> 3))
        folded = dot(turn.astype(BF16), stack.astype(BF16), (1, 0))
        lane = iota((MAIN, TILE), 1)
        notes = []
        for p in range(GROUP):
            at = GROUP * MAIN + p
            notes.append(
                jnp.where(
                    lane == 0,
                    combine[p * MAIN : (p + 1) * MAIN],
                    jnp.where(lane == 1, combine[at : at + 1], 0.0),
                )
            )
        for i, m in enumerate(ms):
            if groups == 1:
                dst = slice(0, m.shape[0])
            at, size = (i, m.shape[0] // MAIN) if groups == 1 else (i * per, per)
            span = slice(at * MAIN, (at + size) * MAIN)
            m[dst, :features] = part[span].astype(BF16)
            m[dst, features : features + fold] = folded[span].astype(BF16)
            m[dst, features + fold :] = jnp.concatenate(notes[at : at + size], axis=0).astype(BF16)
        none = jnp.zeros((pieces, MAIN, hidden), F32)

        def lay(v, place):
            v = v.astype(F32).reshape(pieces, MAIN, hidden)
            both = [v, none] if place == 0 else [none, v]
            return jnp.stack(both, axis=1).reshape(pieces * 2 * MAIN, hidden).astype(BF16)

        hid = [lay(g_gate, 0), lay(g_up, 0), lay(scaled, 1)]
        low, high = rows[:, :half], rows[:, half:]
        keep_ref[all_rows, :] = jnp.where(core == 0, low, high)
        send_ref[all_rows, :half] = jnp.where(core == 0, high, low)
        for i, h in enumerate(hid):
            hid_ref[all_rows, i * hidden : (i + 1) * hidden] = h
            send_ref[all_rows, half + i * hidden : half + (i + 1) * hidden] = h

    if groups == 1:
        work(0)
    else:
        lax.fori_loop(0, groups, lambda g, c: (work(g), c)[1], 0)


def weights_kernel(keep_ref, hid_ref, peer_ref, gate_ref, up_ref, down_ref):
    half = keep_ref.shape[1]
    hidden = gate_ref.shape[0]
    outs = (gate_ref, up_ref, down_ref)
    for i, out in enumerate(outs):
        cols = slice(i * hidden, (i + 1) * hidden)
        far = slice(half + i * hidden, half + (i + 1) * hidden)
        total = dot(hid_ref[:, cols], keep_ref[...], (0, 0))
        total = total + dot(peer_ref[:, far], peer_ref[:, :half], (0, 0))
        out[...] = total.astype(BF16)


def finish_kernel(picks_ref, rank_ref, o0, o1, o2, o3, *rest):
    far, (grad_hbm, comb_hbm, grad_ref, comb_ref, sems) = rest[:-5], rest[-5:]
    window = 1 + len(far)
    quad = lax.axis_index("expert") // SPLIT
    picks = picks_ref[...]
    experts = [quad ^ k for k in range(window)]
    ranks = [rank_ref[k : k + 1, :] for k in range(window)]
    features = grad_ref.shape[1]
    fold = features // MAIN
    toks = picks.shape[1]
    seat = iota((MAIN, toks), 0).astype(F32)
    mains = [(r == seat).astype(F32) for r in ranks]
    lasts = [(r == float(MAIN)).astype(F32) for r in ranks]
    blocks = [(0, o[:MAIN, :].astype(F32)) for o in (o0, o1, o2, o3)]
    blocks += [(1 + k, f[...].astype(F32)) for k, f in enumerate(far)]
    terms = [jnp.zeros((1, toks), F32) for _ in range(window)]
    for k, v in blocks:
        note = v[:, features + fold :]
        terms[k] = terms[k] + jnp.sum(mains[k] * note[:, 0:1], axis=0, keepdims=True)
        terms[k] = terms[k] + lasts[k] * note[0:1, 1:2]
    comb = jnp.zeros(picks.shape, F32)
    for k in range(window):
        comb = comb + jnp.where(picks == experts[k], terms[k], 0.0)
    comb_ref[...] = comb
    stores = [pltpu.make_async_copy(comb_ref, comb_hbm, sems.at[PIECES])]
    stores[0].start()
    row = iota((MAIN, toks), 0)
    each = MAIN // PIECES
    for c in range(MAIN):
        cols = slice(c * fold, (c + 1) * fold)
        left, right = [], []
        for k, v in blocks:
            left += [mains[k], jnp.where(row == c, lasts[k], 0.0)]
            right += [v[:, cols], v[:, features : features + fold]]
        left = jnp.concatenate(left, axis=0).astype(BF16)
        right = jnp.concatenate(right, axis=0).astype(BF16)
        grad_ref[:, cols] = dot(left, right, (0, 0)).astype(BF16)
        if c % each == each - 1:
            done = slice((c + 1 - each) * fold, (c + 1) * fold)
            store = pltpu.make_async_copy(
                grad_ref.at[:, done], grad_hbm.at[:, done], sems.at[c // each]
            )
            store.start()
            stores.append(store)
    for store in stores:
        store.wait()


VM = pl.BlockSpec(memory_space=pltpu.VMEM)
HBM = pl.BlockSpec(memory_space=pltpu.HBM)
ANY = pl.BlockSpec(memory_space=pl.ANY)


def call(kernel, outs, name, args, flops, nbytes, room, specs=None, scratch=(), out_specs=None):
    specs = specs or [VM] * len(args)
    args = [
        pltpu.with_memory_space_constraint(a, pltpu.HBM) if s is HBM else a
        for a, s in zip(args, specs)
    ]
    return pl.pallas_call(
        kernel,
        out_shape=[jax.ShapeDtypeStruct(s, t) for s, t in outs],
        in_specs=specs,
        out_specs=out_specs or [VM] * len(outs),
        scratch_shapes=list(scratch),
        compiler_params=pltpu.CompilerParams(vmem_limit_bytes=min(VMEM_LIMIT, room * MIB)),
        cost_estimate=pl.CostEstimate(flops=flops, bytes_accessed=nbytes, transcendentals=0),
        name=name,
    )(*args)


def swap_by(block, mask):
    count = lax.axis_size("expert")
    return lax.ppermute(block, "expert", [(i, i ^ mask) for i in range(count)])


def body(tokens, out_grad, choices, gates, gate_weight, up_weight, down_weight):
    members = lax.axis_size("expert")
    toks, features = tokens.shape
    hidden = gate_weight.shape[2]
    window = members // SPLIT
    fold = features // MAIN
    half = features // 2
    width = features + fold + TILE
    picks, gates_t = choices.T, gates.T
    wg, wu, wd = gate_weight[0].T, up_weight[0].T, down_weight[0]
    groups = members // GROUP

    *packed, ranks = call(
        pack_kernel,
        [((2 * MAIN, width), BF16)] * window + [((-(-window // 8) * 8, toks), F32)],
        "pack",
        (picks, gates_t, tokens, out_grad),
        2 * (MAIN + 1) * window * toks * features * 2,
        4 * toks * features,
        6 + window,
        [HBM] * 4,
        [pltpu.VMEM(v.shape, v.dtype) for v in (picks, gates_t, tokens, out_grad)]
        + [pltpu.SemaphoreType.DMA((4,))],
    )
    own, others = packed[0], packed[1:]
    arrived = [swap_by(o, SPLIT * (k + 1)) for k, o in enumerate(others)]
    near = [own] + [swap_by(own, j) for j in range(1, SPLIT)]
    held = call(
        fetch_kernel,
        [(wg.shape, BF16), (wu.shape, BF16), ((features, 3 * hidden), BF16)],
        "fetch",
        (wg, wu, wd, near[-1]),
        0,
        6 * features * hidden,
        12,
        [HBM] * 3 + [ANY],
        [pltpu.VMEM(wd.shape, BF16), pltpu.SemaphoreType.DMA((3,))],
    )
    from_far = arrived[0] if window == 2 else jnp.concatenate(arrived, axis=0)
    far = [from_far] + [swap_by(from_far, j) for j in range(1, SPLIT)]
    pairs = list(zip(near, far))
    if groups == 1:
        zs = [z for pair in pairs for z in pair]
    else:
        zs = [jnp.concatenate(pair, axis=0) for pair in pairs]

    all_rows = groups * (GROUP + 1) * 2 * MAIN
    kinds = [((MAIN, width), BF16)] * (GROUP - 2) + [((2 * MAIN, width), BF16)]
    if groups > 1:
        kinds = [((window * MAIN, width), BF16)] * SPLIT
    *messages, keep, hid, send = call(
        functools.partial(expert_kernel, len(zs)),
        kinds
        + [((all_rows, half), BF16), ((all_rows, 3 * hidden), BF16), ((all_rows, half + 3 * hidden), BF16)],
        "expert",
        (*zs, *held),
        2 * all_rows * features * hidden * 5,
        6 * features * hidden,
        10 + 6 * groups,
    )
    if groups == 1:
        home, away = messages[:-1:2], messages[1:-1:2]
    else:
        home, away = [m[:MAIN] for m in messages[:-1]], [m[MAIN:] for m in messages[:-1]]
    both = swap_by(messages[-1], SPLIT - 1)
    back = [away[0]] + [swap_by(away[j], j) for j in range(1, SPLIT - 1)] + [both]
    home = [home[0]] + [swap_by(home[j], j) for j in range(1, SPLIT - 1)]
    send, first = lax.optimization_barrier((send, back[-1]))
    back[-1] = first
    peer = lax.ppermute(send, "dp", [(0, 1), (1, 0)])
    peer, *rest = lax.optimization_barrier((peer, *home[:0:-1]))
    home = home[:1] + rest[::-1]
    gate_grad, up_grad, down_grad = call(
        weights_kernel,
        [((hidden, half), BF16)] * 3,
        "weights",
        (keep, hid, peer),
        2 * 2 * all_rows * half * hidden * 3,
        6 * half * hidden,
        6 + 2 * groups,
    )
    *parts, both = back
    total = sum([b.astype(F32) for b in parts[::-1]], both[MAIN:].astype(F32)).astype(BF16)
    homes = [
        swap_by(total[k * MAIN : (k + 1) * MAIN], SPLIT * (k + 1)) for k in range(window - 1)
    ]
    gate_grad, up_grad, down_grad, *homes = lax.optimization_barrier(
        (gate_grad, up_grad, down_grad, *homes)
    )
    in_grad, combine = call(
        finish_kernel,
        [((toks, features), BF16), ((choices.shape[1], toks), F32)],
        "finish",
        (picks, ranks, *home, both, *homes),
        2 * toks * features * 16 * (SPLIT + window),
        2 * toks * features,
        6 + window,
        scratch=[
            pltpu.VMEM((toks, features), BF16),
            pltpu.VMEM((choices.shape[1], toks), F32),
            pltpu.SemaphoreType.DMA((PIECES + 1,)),
        ],
        out_specs=[HBM, HBM],
    )
    return (
        in_grad,
        combine.T,
        gate_grad.T[None],
        up_grad.T[None],
        down_grad[None],
    )


def solution(mesh):
    return jax.shard_map(
        body,
        mesh=mesh,
        in_specs=(
            P(("groups", "expert", "dp"), None),
            P(("groups", "expert", "dp"), None),
            P(("groups", "expert", "dp"), None),
            P(("groups", "expert", "dp"), None),
            P("expert", None, None),
            P("expert", None, None),
            P("expert", None, None),
        ),
        out_specs=(
            P(("groups", "expert", "dp"), None),
            P(("groups", "expert", "dp"), None),
            P(("groups", "expert"), "dp", None),
            P(("groups", "expert"), "dp", None),
            P(("groups", "expert"), None, "dp"),
        ),
        check_vma=False,
    )
```

```python
import functools

import jax
import jax.numpy as jnp
from jax import lax
from jax.experimental import pallas as pl
from jax.experimental.pallas import tpu as pltpu
from jax.sharding import PartitionSpec as P

SPLIT = 4
MAIN = 8
TILE = 128
PIECES = 4
GROUP = 8
MIB = 1024 * 1024
VMEM_LIMIT = 60 * MIB
F32 = jnp.float32
BF16 = jnp.bfloat16


def iota(shape, axis):
    return lax.broadcasted_iota(jnp.int32, shape, axis)


def dot(a, b, contract):
    return lax.dot_general(a, b, ((contract[:1], contract[1:]), ((), ())), preferred_element_type=F32)


def places(picks, expert):
    named = [jnp.any(picks == e, axis=0, keepdims=True) for e in expert]
    table = jnp.concatenate([n.astype(F32) for n in named], axis=0)
    count, toks = table.shape
    pad = -count % 8
    if pad:
        table = jnp.concatenate([table, jnp.zeros((pad, toks), F32)], axis=0)
    before = (iota((toks, toks), 0) < iota((toks, toks), 1)).astype(BF16)
    rank = dot(table.astype(BF16), before, (1, 0))
    return jnp.where(table > 0, rank, -1.0)


def pack_kernel(picks_hbm, gates_hbm, tok_hbm, grad_hbm, *refs):
    outs, rank_ref = refs[:-6], refs[-6]
    picks_ref, gates_ref, tok_ref, grad_ref, sems = refs[-5:]
    moves = [
        (picks_hbm, picks_ref), (gates_hbm, gates_ref), (tok_hbm, tok_ref), (grad_hbm, grad_ref)
    ]
    loads = [pltpu.make_async_copy(src, dst, sems.at[i]) for i, (src, dst) in enumerate(moves)]
    for load in loads:
        load.start()
    window = len(outs)
    for load in loads[:2]:
        load.wait()
    quad = lax.axis_index("expert") // SPLIT
    picks = picks_ref[...]
    gates = gates_ref[...].astype(F32)
    features = tok_ref.shape[1]
    fold = features // MAIN
    experts = [quad ^ k for k in range(window)]
    table = places(picks, experts)
    rank_ref[...] = table
    ranks = [table[k : k + 1] for k in range(window)]
    toks = picks.shape[1]
    seat = iota((MAIN, toks), 0).astype(F32)
    mains = [(r == seat).astype(F32) for r in ranks]
    last = jnp.concatenate([(r == float(MAIN)).astype(F32) for r in ranks], axis=0)
    pad = -window % 8
    if pad:
        last = jnp.concatenate([last, jnp.zeros((pad, toks), F32)], axis=0)
    choose = jnp.concatenate(mains + [last], axis=0).astype(BF16)
    loads[2].wait()
    tok_rows = dot(choose, tok_ref[...], (1, 0))
    loads[3].wait()
    grad_rows = dot(choose, grad_ref[...], (1, 0))
    row = iota((MAIN, fold), 0)
    lane = iota((MAIN, TILE), 1)
    for k, out in enumerate(outs):
        top = slice(k * MAIN, (k + 1) * MAIN)
        out[:, :features] = jnp.concatenate([tok_rows[top], grad_rows[top]], axis=0).astype(BF16)
        folded = []
        for rows in (tok_rows, grad_rows):
            at = window * MAIN + k
            total = jnp.zeros((MAIN, fold), F32)
            for c in range(MAIN):
                total = jnp.where(row == c, rows[at : at + 1, c * fold : (c + 1) * fold], total)
            folded.append(total)
        out[:, features : features + fold] = jnp.concatenate(folded, axis=0).astype(BF16)
        weight = jnp.sum(jnp.where(picks == experts[k], gates, 0.0), axis=0, keepdims=True)
        seat_gate = jnp.sum(mains[k] * weight, axis=1, keepdims=True)
        last_gate = jnp.sum(last[k : k + 1] * weight, axis=1, keepdims=True)
        tile = jnp.where(lane == 0, seat_gate, jnp.where(lane == 1, last_gate, 0.0))
        out[:, features + fold :] = jnp.concatenate([tile, tile], axis=0).astype(BF16)


def fetch_kernel(gate_hbm, up_hbm, down_hbm, *refs):
    gate_ref, up_ref, across_ref, down_ref, sems = refs[-5:]
    held = (gate_ref, up_ref, down_ref)
    loads = [
        pltpu.make_async_copy(src, dst, sems.at[i])
        for i, (src, dst) in enumerate(zip((gate_hbm, up_hbm, down_hbm), held))
    ]
    for load in loads:
        load.start()
    hidden = gate_ref.shape[0]
    for i, (load, ref) in enumerate(zip(loads, held)):
        load.wait()
        across_ref[:, i * hidden : (i + 1) * hidden] = ref[...].T


def expert_kernel(inputs, *refs):
    wg_ref, wu_ref, across_ref = refs[inputs : inputs + 3]
    zs, ms, (keep_ref, hid_ref, send_ref) = refs[:inputs], refs[inputs + 3 : -3], refs[-3:]
    features = wg_ref.shape[1]
    hidden = wg_ref.shape[0]
    fold = features // MAIN
    half = features // 2
    core = lax.axis_index("dp")
    pair = 2 * MAIN
    per = GROUP // SPLIT
    held = GROUP // len(zs)
    rows_in = held * pair
    groups = zs[0].shape[0] // rows_in

    def work(g):
        if groups == 1:
            src = slice(0, rows_in)
            all_rows = slice(0, (GROUP + 1) * pair)
        else:
            src = pl.ds(pl.multiple_of(g * rows_in, rows_in), rows_in)
            dst = pl.ds(pl.multiple_of(g * per * MAIN, per * MAIN), per * MAIN)
            all_rows = pl.ds(pl.multiple_of(g * (GROUP + 1) * pair, pair), (GROUP + 1) * pair)
        main = [z[src, :features] for z in zs]
        bent = jnp.concatenate([z[src, features : features + fold] for z in zs], axis=0)
        tiles = [z[src, features + fold :].astype(F32) for z in zs]
        n = GROUP * pair
        r, q = iota((n, n), 0), iota((n, n), 1)
        swap = ((r & 8) == (q & 8)) & ((r >> 4) == (q & 7)) & ((r & 7) == (q >> 4))
        flat = dot(swap.astype(BF16), bent, (1, 0)).astype(BF16)
        ninth = jnp.concatenate([flat[c * pair : (c + 1) * pair] for c in range(MAIN)], axis=1)
        rows = jnp.concatenate(main + [ninth], axis=0)
        pre = dot(rows, across_ref[...], (1, 0))
        pre_gate, pre_up, back = (pre[:, i * hidden : (i + 1) * hidden] for i in range(3))
        pieces = GROUP + 1
        upper = lambda v: v.reshape(pieces, 2, MAIN, hidden)[:, 0].reshape(pieces * MAIN, hidden)
        lower = lambda v: v.reshape(pieces, 2, MAIN, hidden)[:, 1].reshape(pieces * MAIN, hidden)
        pre_gate, pre_up, back = upper(pre_gate), upper(pre_up), lower(back)
        columns = []
        last = jnp.zeros((MAIN, 1), F32)
        seat = iota((MAIN, 1), 0)
        for p in range(GROUP):
            tile = tiles[p // held][(p % held) * pair : (p % held) * pair + MAIN]
            columns.append(tile[:, 0:1])
            last = jnp.where(seat == p, tile[:, 1:2], last)
        gate = jnp.concatenate(columns + [last], axis=0)
        sig = 1.0 / (1.0 + jnp.exp(-pre_gate))
        silu = pre_gate * sig
        slope = sig * (1.0 + pre_gate * (1.0 - sig))
        act = silu * pre_up
        combine = jnp.sum(back * act, axis=1, keepdims=True)
        scaled = gate * act
        gated = gate * back
        g_gate = (gated * slope * pre_up).astype(BF16)
        g_up = (gated * silu).astype(BF16)
        part = dot(g_gate, wg_ref[...], (1, 0)) + dot(g_up, wu_ref[...], (1, 0))
        tail = part[GROUP * MAIN :].astype(BF16).astype(F32)
        stack = jnp.concatenate([tail[:, c * fold : (c + 1) * fold] for c in range(MAIN)], axis=0)
        n = GROUP * MAIN
        r, q = iota((n, n), 0), iota((n, n), 1)
        turn = ((r >> 3) == (q & 7)) & ((r & 7) == (q >> 3))
        folded = dot(turn.astype(BF16), stack.astype(BF16), (1, 0))
        lane = iota((MAIN, TILE), 1)
        notes = []
        for p in range(GROUP):
            at = GROUP * MAIN + p
            notes.append(
                jnp.where(
                    lane == 0,
                    combine[p * MAIN : (p + 1) * MAIN],
                    jnp.where(lane == 1, combine[at : at + 1], 0.0),
                )
            )
        for i, m in enumerate(ms):
            if groups == 1:
                dst = slice(0, m.shape[0])
            at, size = (i, m.shape[0] // MAIN) if groups == 1 else (i * per, per)
            span = slice(at * MAIN, (at + size) * MAIN)
            m[dst, :features] = part[span].astype(BF16)
            m[dst, features : features + fold] = folded[span].astype(BF16)
            m[dst, features + fold :] = jnp.concatenate(notes[at : at + size], axis=0).astype(BF16)
        none = jnp.zeros((pieces, MAIN, hidden), F32)

        def lay(v, place):
            v = v.astype(F32).reshape(pieces, MAIN, hidden)
            both = [v, none] if place == 0 else [none, v]
            return jnp.stack(both, axis=1).reshape(pieces * 2 * MAIN, hidden).astype(BF16)

        hid = [lay(g_gate, 0), lay(g_up, 0), lay(scaled, 1)]
        low, high = rows[:, :half], rows[:, half:]
        keep_ref[all_rows, :] = jnp.where(core == 0, low, high)
        send_ref[all_rows, :half] = jnp.where(core == 0, high, low)
        for i, h in enumerate(hid):
            hid_ref[all_rows, i * hidden : (i + 1) * hidden] = h
            send_ref[all_rows, half + i * hidden : half + (i + 1) * hidden] = h

    if groups == 1:
        work(0)
    else:
        lax.fori_loop(0, groups, lambda g, c: (work(g), c)[1], 0)


def weights_kernel(keep_ref, hid_ref, peer_ref, gate_ref, up_ref, down_ref):
    half = keep_ref.shape[1]
    hidden = gate_ref.shape[0]
    outs = (gate_ref, up_ref, down_ref)
    for i, out in enumerate(outs):
        cols = slice(i * hidden, (i + 1) * hidden)
        far = slice(half + i * hidden, half + (i + 1) * hidden)
        total = dot(hid_ref[:, cols], keep_ref[...], (0, 0))
        total = total + dot(peer_ref[:, far], peer_ref[:, :half], (0, 0))
        out[...] = total.astype(BF16)


def finish_kernel(picks_ref, rank_ref, o0, o1, o2, o3, *rest):
    far, (grad_hbm, comb_hbm, grad_ref, comb_ref, sems) = rest[:-5], rest[-5:]
    window = 1 + len(far)
    quad = lax.axis_index("expert") // SPLIT
    picks = picks_ref[...]
    experts = [quad ^ k for k in range(window)]
    ranks = [rank_ref[k : k + 1, :] for k in range(window)]
    features = grad_ref.shape[1]
    fold = features // MAIN
    toks = picks.shape[1]
    seat = iota((MAIN, toks), 0).astype(F32)
    mains = [(r == seat).astype(F32) for r in ranks]
    lasts = [(r == float(MAIN)).astype(F32) for r in ranks]
    blocks = [(0, o[:MAIN, :].astype(F32)) for o in (o0, o1, o2, o3)]
    blocks += [(1 + k, f[...].astype(F32)) for k, f in enumerate(far)]
    terms = [jnp.zeros((1, toks), F32) for _ in range(window)]
    for k, v in blocks:
        note = v[:, features + fold :]
        terms[k] = terms[k] + jnp.sum(mains[k] * note[:, 0:1], axis=0, keepdims=True)
        terms[k] = terms[k] + lasts[k] * note[0:1, 1:2]
    comb = jnp.zeros(picks.shape, F32)
    for k in range(window):
        comb = comb + jnp.where(picks == experts[k], terms[k], 0.0)
    comb_ref[...] = comb
    stores = [pltpu.make_async_copy(comb_ref, comb_hbm, sems.at[PIECES])]
    stores[0].start()
    row = iota((MAIN, toks), 0)
    each = MAIN // PIECES
    for c in range(MAIN):
        cols = slice(c * fold, (c + 1) * fold)
        left, right = [], []
        for k, v in blocks:
            left += [mains[k], jnp.where(row == c, lasts[k], 0.0)]
            right += [v[:, cols], v[:, features : features + fold]]
        left = jnp.concatenate(left, axis=0).astype(BF16)
        right = jnp.concatenate(right, axis=0).astype(BF16)
        grad_ref[:, cols] = dot(left, right, (0, 0)).astype(BF16)
        if c % each == each - 1:
            done = slice((c + 1 - each) * fold, (c + 1) * fold)
            store = pltpu.make_async_copy(
                grad_ref.at[:, done], grad_hbm.at[:, done], sems.at[c // each]
            )
            store.start()
            stores.append(store)
    for store in stores:
        store.wait()


VM = pl.BlockSpec(memory_space=pltpu.VMEM)
HBM = pl.BlockSpec(memory_space=pltpu.HBM)
ANY = pl.BlockSpec(memory_space=pl.ANY)


def call(kernel, outs, name, args, flops, nbytes, room, specs=None, scratch=(), out_specs=None):
    specs = specs or [VM] * len(args)
    args = [
        pltpu.with_memory_space_constraint(a, pltpu.HBM) if s is HBM else a
        for a, s in zip(args, specs)
    ]
    return pl.pallas_call(
        kernel,
        out_shape=[jax.ShapeDtypeStruct(s, t) for s, t in outs],
        in_specs=specs,
        out_specs=out_specs or [VM] * len(outs),
        scratch_shapes=list(scratch),
        compiler_params=pltpu.CompilerParams(vmem_limit_bytes=min(VMEM_LIMIT, room * MIB)),
        cost_estimate=pl.CostEstimate(flops=flops, bytes_accessed=nbytes, transcendentals=0),
        name=name,
    )(*args)


def swap_by(block, mask):
    count = lax.axis_size("expert")
    return lax.ppermute(block, "expert", [(i, i ^ mask) for i in range(count)])


def body(tokens, out_grad, choices, gates, gate_weight, up_weight, down_weight):
    members = lax.axis_size("expert")
    toks, features = tokens.shape
    hidden = gate_weight.shape[2]
    window = members // SPLIT
    fold = features // MAIN
    half = features // 2
    width = features + fold + TILE
    picks, gates_t = choices.T, gates.T
    wg, wu, wd = gate_weight[0].T, up_weight[0].T, down_weight[0]
    groups = members // GROUP

    *packed, ranks = call(
        pack_kernel,
        [((2 * MAIN, width), BF16)] * window + [((-(-window // 8) * 8, toks), F32)],
        "pack",
        (picks, gates_t, tokens, out_grad),
        2 * (MAIN + 1) * window * toks * features * 2,
        4 * toks * features,
        6 + window,
        [HBM] * 4,
        [pltpu.VMEM(v.shape, v.dtype) for v in (picks, gates_t, tokens, out_grad)]
        + [pltpu.SemaphoreType.DMA((4,))],
    )
    own, others = packed[0], packed[1:]
    arrived = [swap_by(o, SPLIT * (k + 1)) for k, o in enumerate(others)]
    near = [own] + [swap_by(own, j) for j in range(1, SPLIT)]
    held = call(
        fetch_kernel,
        [(wg.shape, BF16), (wu.shape, BF16), ((features, 3 * hidden), BF16)],
        "fetch",
        (wg, wu, wd, near[1]),
        0,
        6 * features * hidden,
        12,
        [HBM] * 3 + [ANY],
        [pltpu.VMEM(wd.shape, BF16), pltpu.SemaphoreType.DMA((3,))],
    )
    from_far = arrived[0] if window == 2 else jnp.concatenate(arrived, axis=0)
    far = [from_far] + [swap_by(from_far, j) for j in range(1, SPLIT)]
    pairs = list(zip(near, far))
    if groups == 1:
        zs = [z for pair in pairs for z in pair]
    else:
        zs = [jnp.concatenate(pair, axis=0) for pair in pairs]

    all_rows = groups * (GROUP + 1) * 2 * MAIN
    kinds = [((MAIN, width), BF16)] * (GROUP - 2) + [((2 * MAIN, width), BF16)]
    if groups > 1:
        kinds = [((window * MAIN, width), BF16)] * SPLIT
    *messages, keep, hid, send = call(
        functools.partial(expert_kernel, len(zs)),
        kinds
        + [((all_rows, half), BF16), ((all_rows, 3 * hidden), BF16), ((all_rows, half + 3 * hidden), BF16)],
        "expert",
        (*zs, *held),
        2 * all_rows * features * hidden * 5,
        6 * features * hidden,
        10 + 6 * groups,
    )
    if groups == 1:
        home, away = messages[:-1:2], messages[1:-1:2]
    else:
        home, away = [m[:MAIN] for m in messages[:-1]], [m[MAIN:] for m in messages[:-1]]
    both = swap_by(messages[-1], SPLIT - 1)
    back = [away[0]] + [swap_by(away[j], j) for j in range(1, SPLIT - 1)] + [both]
    home = [home[0]] + [swap_by(home[j], j) for j in range(1, SPLIT - 1)]
    send, first = lax.optimization_barrier((send, back[-1]))
    back[-1] = first
    peer = lax.ppermute(send, "dp", [(0, 1), (1, 0)])
    peer, *rest = lax.optimization_barrier((peer, *home[:0:-1]))
    home = home[:1] + rest[::-1]
    gate_grad, up_grad, down_grad = call(
        weights_kernel,
        [((hidden, half), BF16)] * 3,
        "weights",
        (keep, hid, peer),
        2 * 2 * all_rows * half * hidden * 3,
        6 * half * hidden,
        6 + 2 * groups,
    )
    *parts, both = back
    total = sum([b.astype(F32) for b in parts[::-1]], both[MAIN:].astype(F32)).astype(BF16)
    homes = [
        swap_by(total[k * MAIN : (k + 1) * MAIN], SPLIT * (k + 1)) for k in range(window - 1)
    ]
    gate_grad, up_grad, down_grad, *homes = lax.optimization_barrier(
        (gate_grad, up_grad, down_grad, *homes)
    )
    in_grad, combine = call(
        finish_kernel,
        [((toks, features), BF16), ((choices.shape[1], toks), F32)],
        "finish",
        (picks, ranks, *home, both, *homes),
        2 * toks * features * 16 * (SPLIT + window),
        2 * toks * features,
        6 + window,
        scratch=[
            pltpu.VMEM((toks, features), BF16),
            pltpu.VMEM((choices.shape[1], toks), F32),
            pltpu.SemaphoreType.DMA((PIECES + 1,)),
        ],
        out_specs=[HBM, HBM],
    )
    return (
        in_grad,
        combine.T,
        gate_grad.T[None],
        up_grad.T[None],
        down_grad[None],
    )


def solution(mesh):
    return jax.shard_map(
        body,
        mesh=mesh,
        in_specs=(
            P(("groups", "expert", "dp"), None),
            P(("groups", "expert", "dp"), None),
            P(("groups", "expert", "dp"), None),
            P(("groups", "expert", "dp"), None),
            P("expert", None, None),
            P("expert", None, None),
            P("expert", None, None),
        ),
        out_specs=(
            P(("groups", "expert", "dp"), None),
            P(("groups", "expert", "dp"), None),
            P(("groups", "expert"), "dp", None),
            P(("groups", "expert"), "dp", None),
            P(("groups", "expert"), None, "dp"),
        ),
        check_vma=False,
    )
```

```python
import functools

import jax
import jax.numpy as jnp
from jax import lax
from jax.experimental import pallas as pl
from jax.experimental.pallas import tpu as pltpu
from jax.sharding import PartitionSpec as P

SPLIT = 4
MAIN = 8
TILE = 128
PIECES = 4
GROUP = 8
MIB = 1024 * 1024
VMEM_LIMIT = 60 * MIB
F32 = jnp.float32
BF16 = jnp.bfloat16


def iota(shape, axis):
    return lax.broadcasted_iota(jnp.int32, shape, axis)


def dot(a, b, contract):
    return lax.dot_general(a, b, ((contract[:1], contract[1:]), ((), ())), preferred_element_type=F32)


def places(picks, expert):
    named = [jnp.any(picks == e, axis=0, keepdims=True) for e in expert]
    table = jnp.concatenate([n.astype(F32) for n in named], axis=0)
    count, toks = table.shape
    pad = -count % 8
    if pad:
        table = jnp.concatenate([table, jnp.zeros((pad, toks), F32)], axis=0)
    before = (iota((toks, toks), 0) < iota((toks, toks), 1)).astype(BF16)
    rank = dot(table.astype(BF16), before, (1, 0))
    return jnp.where(table > 0, rank, -1.0)


def pack_kernel(picks_hbm, gates_hbm, tok_hbm, grad_hbm, *refs):
    outs, rank_ref = refs[:-6], refs[-6]
    picks_ref, gates_ref, tok_ref, grad_ref, sems = refs[-5:]
    moves = [
        (picks_hbm, picks_ref), (gates_hbm, gates_ref), (tok_hbm, tok_ref), (grad_hbm, grad_ref)
    ]
    loads = [pltpu.make_async_copy(src, dst, sems.at[i]) for i, (src, dst) in enumerate(moves)]
    for load in loads:
        load.start()
    window = len(outs)
    for load in loads[:2]:
        load.wait()
    quad = lax.axis_index("expert") // SPLIT
    picks = picks_ref[...]
    gates = gates_ref[...].astype(F32)
    features = tok_ref.shape[1]
    fold = features // MAIN
    experts = [quad ^ k for k in range(window)]
    table = places(picks, experts)
    rank_ref[...] = table
    ranks = [table[k : k + 1] for k in range(window)]
    toks = picks.shape[1]
    seat = iota((MAIN, toks), 0).astype(F32)
    mains = [(r == seat).astype(F32) for r in ranks]
    last = jnp.concatenate([(r == float(MAIN)).astype(F32) for r in ranks], axis=0)
    pad = -window % 8
    if pad:
        last = jnp.concatenate([last, jnp.zeros((pad, toks), F32)], axis=0)
    choose = jnp.concatenate(mains + [last], axis=0).astype(BF16)
    loads[2].wait()
    tok_rows = dot(choose, tok_ref[...], (1, 0))
    loads[3].wait()
    grad_rows = dot(choose, grad_ref[...], (1, 0))
    row = iota((MAIN, fold), 0)
    lane = iota((MAIN, TILE), 1)
    for k, out in enumerate(outs):
        top = slice(k * MAIN, (k + 1) * MAIN)
        out[:, :features] = jnp.concatenate([tok_rows[top], grad_rows[top]], axis=0).astype(BF16)
        folded = []
        for rows in (tok_rows, grad_rows):
            at = window * MAIN + k
            total = jnp.zeros((MAIN, fold), F32)
            for c in range(MAIN):
                total = jnp.where(row == c, rows[at : at + 1, c * fold : (c + 1) * fold], total)
            folded.append(total)
        out[:, features : features + fold] = jnp.concatenate(folded, axis=0).astype(BF16)
        weight = jnp.sum(jnp.where(picks == experts[k], gates, 0.0), axis=0, keepdims=True)
        seat_gate = jnp.sum(mains[k] * weight, axis=1, keepdims=True)
        last_gate = jnp.sum(last[k : k + 1] * weight, axis=1, keepdims=True)
        tile = jnp.where(lane == 0, seat_gate, jnp.where(lane == 1, last_gate, 0.0))
        out[:, features + fold :] = jnp.concatenate([tile, tile], axis=0).astype(BF16)


def fetch_kernel(gate_hbm, up_hbm, down_hbm, *refs):
    gate_ref, up_ref, across_ref, down_ref, sems = refs[-5:]
    held = (gate_ref, up_ref, down_ref)
    loads = [
        pltpu.make_async_copy(src, dst, sems.at[i])
        for i, (src, dst) in enumerate(zip((gate_hbm, up_hbm, down_hbm), held))
    ]
    for load in loads:
        load.start()
    hidden = gate_ref.shape[0]
    for i, (load, ref) in enumerate(zip(loads, held)):
        load.wait()
        across_ref[:, i * hidden : (i + 1) * hidden] = ref[...].T


def expert_kernel(inputs, *refs):
    wg_ref, wu_ref, across_ref = refs[inputs : inputs + 3]
    zs, ms, (keep_ref, hid_ref, send_ref) = refs[:inputs], refs[inputs + 3 : -3], refs[-3:]
    features = wg_ref.shape[1]
    hidden = wg_ref.shape[0]
    fold = features // MAIN
    half = features // 2
    core = lax.axis_index("dp")
    pair = 2 * MAIN
    per = GROUP // SPLIT
    held = GROUP // len(zs)
    rows_in = held * pair
    groups = zs[0].shape[0] // rows_in

    def work(g):
        if groups == 1:
            src = slice(0, rows_in)
            all_rows = slice(0, (GROUP + 1) * pair)
        else:
            src = pl.ds(pl.multiple_of(g * rows_in, rows_in), rows_in)
            dst = pl.ds(pl.multiple_of(g * per * MAIN, per * MAIN), per * MAIN)
            all_rows = pl.ds(pl.multiple_of(g * (GROUP + 1) * pair, pair), (GROUP + 1) * pair)
        main = [z[src, :features] for z in zs]
        bent = jnp.concatenate([z[src, features : features + fold] for z in zs], axis=0)
        tiles = [z[src, features + fold :].astype(F32) for z in zs]
        n = GROUP * pair
        r, q = iota((n, n), 0), iota((n, n), 1)
        swap = ((r & 8) == (q & 8)) & ((r >> 4) == (q & 7)) & ((r & 7) == (q >> 4))
        flat = dot(swap.astype(BF16), bent, (1, 0)).astype(BF16)
        ninth = jnp.concatenate([flat[c * pair : (c + 1) * pair] for c in range(MAIN)], axis=1)
        rows = jnp.concatenate(main + [ninth], axis=0)
        pre = dot(rows, across_ref[...], (1, 0))
        pre_gate, pre_up, back = (pre[:, i * hidden : (i + 1) * hidden] for i in range(3))
        pieces = GROUP + 1
        upper = lambda v: v.reshape(pieces, 2, MAIN, hidden)[:, 0].reshape(pieces * MAIN, hidden)
        lower = lambda v: v.reshape(pieces, 2, MAIN, hidden)[:, 1].reshape(pieces * MAIN, hidden)
        pre_gate, pre_up, back = upper(pre_gate), upper(pre_up), lower(back)
        columns = []
        last = jnp.zeros((MAIN, 1), F32)
        seat = iota((MAIN, 1), 0)
        for p in range(GROUP):
            tile = tiles[p // held][(p % held) * pair : (p % held) * pair + MAIN]
            columns.append(tile[:, 0:1])
            last = jnp.where(seat == p, tile[:, 1:2], last)
        gate = jnp.concatenate(columns + [last], axis=0)
        sig = 1.0 / (1.0 + jnp.exp(-pre_gate))
        silu = pre_gate * sig
        slope = sig * (1.0 + pre_gate * (1.0 - sig))
        act = silu * pre_up
        combine = jnp.sum(back * act, axis=1, keepdims=True)
        scaled = gate * act
        gated = gate * back
        g_gate = (gated * slope * pre_up).astype(BF16)
        g_up = (gated * silu).astype(BF16)
        part = dot(g_gate, wg_ref[...], (1, 0)) + dot(g_up, wu_ref[...], (1, 0))
        tail = part[GROUP * MAIN :].astype(BF16).astype(F32)
        stack = jnp.concatenate([tail[:, c * fold : (c + 1) * fold] for c in range(MAIN)], axis=0)
        n = GROUP * MAIN
        r, q = iota((n, n), 0), iota((n, n), 1)
        turn = ((r >> 3) == (q & 7)) & ((r & 7) == (q >> 3))
        folded = dot(turn.astype(BF16), stack.astype(BF16), (1, 0))
        lane = iota((MAIN, TILE), 1)
        notes = []
        for p in range(GROUP):
            at = GROUP * MAIN + p
            notes.append(
                jnp.where(
                    lane == 0,
                    combine[p * MAIN : (p + 1) * MAIN],
                    jnp.where(lane == 1, combine[at : at + 1], 0.0),
                )
            )
        for i, m in enumerate(ms):
            if groups == 1:
                dst = slice(0, m.shape[0])
            at, size = (i, m.shape[0] // MAIN) if groups == 1 else (i * per, per)
            span = slice(at * MAIN, (at + size) * MAIN)
            m[dst, :features] = part[span].astype(BF16)
            m[dst, features : features + fold] = folded[span].astype(BF16)
            m[dst, features + fold :] = jnp.concatenate(notes[at : at + size], axis=0).astype(BF16)
        none = jnp.zeros((pieces, MAIN, hidden), F32)

        def lay(v, place):
            v = v.astype(F32).reshape(pieces, MAIN, hidden)
            both = [v, none] if place == 0 else [none, v]
            return jnp.stack(both, axis=1).reshape(pieces * 2 * MAIN, hidden).astype(BF16)

        hid = [lay(g_gate, 0), lay(g_up, 0), lay(scaled, 1)]
        low, high = rows[:, :half], rows[:, half:]
        keep_ref[all_rows, :] = jnp.where(core == 0, low, high)
        send_ref[all_rows, :half] = jnp.where(core == 0, high, low)
        for i, h in enumerate(hid):
            hid_ref[all_rows, i * hidden : (i + 1) * hidden] = h
            send_ref[all_rows, half + i * hidden : half + (i + 1) * hidden] = h

    if groups == 1:
        work(0)
    else:
        lax.fori_loop(0, groups, lambda g, c: (work(g), c)[1], 0)


def weights_kernel(keep_ref, hid_ref, peer_ref, gate_ref, up_ref, down_ref):
    half = keep_ref.shape[1]
    hidden = gate_ref.shape[0]
    outs = (gate_ref, up_ref, down_ref)
    for i, out in enumerate(outs):
        cols = slice(i * hidden, (i + 1) * hidden)
        far = slice(half + i * hidden, half + (i + 1) * hidden)
        total = dot(hid_ref[:, cols], keep_ref[...], (0, 0))
        total = total + dot(peer_ref[:, far], peer_ref[:, :half], (0, 0))
        out[...] = total.astype(BF16)


def finish_kernel(picks_ref, rank_ref, o0, o1, o2, o3, *rest):
    far, (grad_hbm, comb_hbm, grad_ref, comb_ref, sems) = rest[:-5], rest[-5:]
    window = 1 + len(far)
    quad = lax.axis_index("expert") // SPLIT
    picks = picks_ref[...]
    experts = [quad ^ k for k in range(window)]
    ranks = [rank_ref[k : k + 1, :] for k in range(window)]
    features = grad_ref.shape[1]
    fold = features // MAIN
    toks = picks.shape[1]
    seat = iota((MAIN, toks), 0).astype(F32)
    mains = [(r == seat).astype(F32) for r in ranks]
    lasts = [(r == float(MAIN)).astype(F32) for r in ranks]
    blocks = [(0, o[:MAIN, :].astype(F32)) for o in (o0, o1, o2, o3)]
    blocks += [(1 + k, f[...].astype(F32)) for k, f in enumerate(far)]
    terms = [jnp.zeros((1, toks), F32) for _ in range(window)]
    for k, v in blocks:
        note = v[:, features + fold :]
        terms[k] = terms[k] + jnp.sum(mains[k] * note[:, 0:1], axis=0, keepdims=True)
        terms[k] = terms[k] + lasts[k] * note[0:1, 1:2]
    comb = jnp.zeros(picks.shape, F32)
    for k in range(window):
        comb = comb + jnp.where(picks == experts[k], terms[k], 0.0)
    comb_ref[...] = comb
    stores = [pltpu.make_async_copy(comb_ref, comb_hbm, sems.at[PIECES])]
    stores[0].start()
    row = iota((MAIN, toks), 0)
    each = MAIN // PIECES
    for c in range(MAIN):
        cols = slice(c * fold, (c + 1) * fold)
        left, right = [], []
        for k, v in blocks:
            left += [mains[k], jnp.where(row == c, lasts[k], 0.0)]
            right += [v[:, cols], v[:, features : features + fold]]
        left = jnp.concatenate(left, axis=0).astype(BF16)
        right = jnp.concatenate(right, axis=0).astype(BF16)
        grad_ref[:, cols] = dot(left, right, (0, 0)).astype(BF16)
        if c % each == each - 1:
            done = slice((c + 1 - each) * fold, (c + 1) * fold)
            store = pltpu.make_async_copy(
                grad_ref.at[:, done], grad_hbm.at[:, done], sems.at[c // each]
            )
            store.start()
            stores.append(store)
    for store in stores:
        store.wait()


VM = pl.BlockSpec(memory_space=pltpu.VMEM)
HBM = pl.BlockSpec(memory_space=pltpu.HBM)
ANY = pl.BlockSpec(memory_space=pl.ANY)


def call(kernel, outs, name, args, flops, nbytes, room, specs=None, scratch=(), out_specs=None):
    specs = specs or [VM] * len(args)
    args = [
        pltpu.with_memory_space_constraint(a, pltpu.HBM) if s is HBM else a
        for a, s in zip(args, specs)
    ]
    return pl.pallas_call(
        kernel,
        out_shape=[jax.ShapeDtypeStruct(s, t) for s, t in outs],
        in_specs=specs,
        out_specs=out_specs or [VM] * len(outs),
        scratch_shapes=list(scratch),
        compiler_params=pltpu.CompilerParams(vmem_limit_bytes=min(VMEM_LIMIT, room * MIB)),
        cost_estimate=pl.CostEstimate(flops=flops, bytes_accessed=nbytes, transcendentals=0),
        name=name,
    )(*args)


def swap_by(block, mask):
    count = lax.axis_size("expert")
    return lax.ppermute(block, "expert", [(i, i ^ mask) for i in range(count)])


def body(tokens, out_grad, choices, gates, gate_weight, up_weight, down_weight):
    members = lax.axis_size("expert")
    toks, features = tokens.shape
    hidden = gate_weight.shape[2]
    window = members // SPLIT
    fold = features // MAIN
    half = features // 2
    width = features + fold + TILE
    picks, gates_t = choices.T, gates.T
    wg, wu, wd = gate_weight[0].T, up_weight[0].T, down_weight[0]
    groups = members // GROUP

    *packed, ranks = call(
        pack_kernel,
        [((2 * MAIN, width), BF16)] * window + [((-(-window // 8) * 8, toks), F32)],
        "pack",
        (picks, gates_t, tokens, out_grad),
        2 * (MAIN + 1) * window * toks * features * 2,
        4 * toks * features,
        6 + window,
        [HBM] * 4,
        [pltpu.VMEM(v.shape, v.dtype) for v in (picks, gates_t, tokens, out_grad)]
        + [pltpu.SemaphoreType.DMA((4,))],
    )
    own, others = packed[0], packed[1:]
    arrived = [swap_by(o, SPLIT * (k + 1)) for k, o in enumerate(others)]
    near = [own] + [swap_by(own, j) for j in range(1, SPLIT)]
    held = call(
        fetch_kernel,
        [(wg.shape, BF16), (wu.shape, BF16), ((features, 3 * hidden), BF16)],
        "fetch",
        (wg, wu, wd, near[1]),
        0,
        6 * features * hidden,
        12,
        [HBM] * 3 + [ANY],
        [pltpu.VMEM(wd.shape, BF16), pltpu.SemaphoreType.DMA((3,))],
    )
    from_far = arrived[0] if window == 2 else jnp.concatenate(arrived, axis=0)
    far = [from_far] + [swap_by(from_far, j) for j in range(1, SPLIT)]
    pairs = list(zip(near, far))
    if groups == 1:
        zs = [z for pair in pairs for z in pair]
    else:
        zs = [jnp.concatenate(pair, axis=0) for pair in pairs]

    all_rows = groups * (GROUP + 1) * 2 * MAIN
    kinds = [((MAIN, width), BF16)] * (GROUP - 2) + [((2 * MAIN, width), BF16)]
    if groups > 1:
        kinds = [((window * MAIN, width), BF16)] * SPLIT
    *messages, keep, hid, send = call(
        functools.partial(expert_kernel, len(zs)),
        kinds
        + [((all_rows, half), BF16), ((all_rows, 3 * hidden), BF16), ((all_rows, half + 3 * hidden), BF16)],
        "expert",
        (*zs, *held),
        2 * all_rows * features * hidden * 5,
        6 * features * hidden,
        10 + 6 * groups,
    )
    if groups == 1:
        home, away = messages[:-1:2], messages[1:-1:2]
    else:
        home, away = [m[:MAIN] for m in messages[:-1]], [m[MAIN:] for m in messages[:-1]]
    both = swap_by(messages[-1], SPLIT - 1)
    back = [away[0]] + [swap_by(away[j], j) for j in range(1, SPLIT - 1)] + [both]
    home = [home[0]] + [swap_by(home[j], j) for j in range(1, SPLIT - 1)]
    send, first = lax.optimization_barrier((send, back[2]))
    back[2] = first
    peer = lax.ppermute(send, "dp", [(0, 1), (1, 0)])
    peer, *rest = lax.optimization_barrier((peer, *home[:0:-1]))
    home = home[:1] + rest[::-1]
    gate_grad, up_grad, down_grad = call(
        weights_kernel,
        [((hidden, half), BF16)] * 3,
        "weights",
        (keep, hid, peer),
        2 * 2 * all_rows * half * hidden * 3,
        6 * half * hidden,
        6 + 2 * groups,
    )
    *parts, both = back
    total = sum([b.astype(F32) for b in parts[::-1]], both[MAIN:].astype(F32)).astype(BF16)
    homes = [
        swap_by(total[k * MAIN : (k + 1) * MAIN], SPLIT * (k + 1)) for k in range(window - 1)
    ]
    gate_grad, up_grad, down_grad, *homes = lax.optimization_barrier(
        (gate_grad, up_grad, down_grad, *homes)
    )
    in_grad, combine = call(
        finish_kernel,
        [((toks, features), BF16), ((choices.shape[1], toks), F32)],
        "finish",
        (picks, ranks, *home, both, *homes),
        2 * toks * features * 16 * (SPLIT + window),
        2 * toks * features,
        6 + window,
        scratch=[
            pltpu.VMEM((toks, features), BF16),
            pltpu.VMEM((choices.shape[1], toks), F32),
            pltpu.SemaphoreType.DMA((PIECES + 1,)),
        ],
        out_specs=[HBM, HBM],
    )
    return (
        in_grad,
        combine.T,
        gate_grad.T[None],
        up_grad.T[None],
        down_grad[None],
    )


def solution(mesh):
    return jax.shard_map(
        body,
        mesh=mesh,
        in_specs=(
            P(("groups", "expert", "dp"), None),
            P(("groups", "expert", "dp"), None),
            P(("groups", "expert", "dp"), None),
            P(("groups", "expert", "dp"), None),
            P("expert", None, None),
            P("expert", None, None),
            P("expert", None, None),
        ),
        out_specs=(
            P(("groups", "expert", "dp"), None),
            P(("groups", "expert", "dp"), None),
            P(("groups", "expert"), "dp", None),
            P(("groups", "expert"), "dp", None),
            P(("groups", "expert"), None, "dp"),
        ),
        check_vma=False,
    )
```

```python
import functools

import jax
import jax.numpy as jnp
from jax import lax
from jax.experimental import pallas as pl
from jax.experimental.pallas import tpu as pltpu
from jax.sharding import PartitionSpec as P

SPLIT = 4
MAIN = 8
TILE = 128
PIECES = 4
GROUP = 8
MIB = 1024 * 1024
VMEM_LIMIT = 60 * MIB
F32 = jnp.float32
BF16 = jnp.bfloat16


def iota(shape, axis):
    return lax.broadcasted_iota(jnp.int32, shape, axis)


def dot(a, b, contract):
    return lax.dot_general(a, b, ((contract[:1], contract[1:]), ((), ())), preferred_element_type=F32)


def places(picks, expert):
    named = [jnp.any(picks == e, axis=0, keepdims=True) for e in expert]
    table = jnp.concatenate([n.astype(F32) for n in named], axis=0)
    count, toks = table.shape
    pad = -count % 8
    if pad:
        table = jnp.concatenate([table, jnp.zeros((pad, toks), F32)], axis=0)
    before = (iota((toks, toks), 0) < iota((toks, toks), 1)).astype(BF16)
    rank = dot(table.astype(BF16), before, (1, 0))
    return jnp.where(table > 0, rank, -1.0)


def pack_kernel(picks_hbm, gates_hbm, tok_hbm, grad_hbm, *refs):
    outs, rank_ref = refs[:-6], refs[-6]
    picks_ref, gates_ref, tok_ref, grad_ref, sems = refs[-5:]
    moves = [
        (picks_hbm, picks_ref), (gates_hbm, gates_ref), (tok_hbm, tok_ref), (grad_hbm, grad_ref)
    ]
    loads = [pltpu.make_async_copy(src, dst, sems.at[i]) for i, (src, dst) in enumerate(moves)]
    for load in loads:
        load.start()
    window = len(outs)
    for load in loads[:2]:
        load.wait()
    quad = lax.axis_index("expert") // SPLIT
    picks = picks_ref[...]
    gates = gates_ref[...].astype(F32)
    features = tok_ref.shape[1]
    fold = features // MAIN
    experts = [quad ^ k for k in range(window)]
    table = places(picks, experts)
    rank_ref[...] = table
    ranks = [table[k : k + 1] for k in range(window)]
    toks = picks.shape[1]
    seat = iota((MAIN, toks), 0).astype(F32)
    mains = [(r == seat).astype(F32) for r in ranks]
    last = jnp.concatenate([(r == float(MAIN)).astype(F32) for r in ranks], axis=0)
    pad = -window % 8
    if pad:
        last = jnp.concatenate([last, jnp.zeros((pad, toks), F32)], axis=0)
    choose = jnp.concatenate(mains + [last], axis=0).astype(BF16)
    loads[2].wait()
    tok_rows = dot(choose, tok_ref[...], (1, 0))
    loads[3].wait()
    grad_rows = dot(choose, grad_ref[...], (1, 0))
    row = iota((MAIN, fold), 0)
    lane = iota((MAIN, TILE), 1)
    for k, out in enumerate(outs):
        top = slice(k * MAIN, (k + 1) * MAIN)
        out[:, :features] = jnp.concatenate([tok_rows[top], grad_rows[top]], axis=0).astype(BF16)
        folded = []
        for rows in (tok_rows, grad_rows):
            at = window * MAIN + k
            total = jnp.zeros((MAIN, fold), F32)
            for c in range(MAIN):
                total = jnp.where(row == c, rows[at : at + 1, c * fold : (c + 1) * fold], total)
            folded.append(total)
        out[:, features : features + fold] = jnp.concatenate(folded, axis=0).astype(BF16)
        weight = jnp.sum(jnp.where(picks == experts[k], gates, 0.0), axis=0, keepdims=True)
        seat_gate = jnp.sum(mains[k] * weight, axis=1, keepdims=True)
        last_gate = jnp.sum(last[k : k + 1] * weight, axis=1, keepdims=True)
        tile = jnp.where(lane == 0, seat_gate, jnp.where(lane == 1, last_gate, 0.0))
        out[:, features + fold :] = jnp.concatenate([tile, tile], axis=0).astype(BF16)


def fetch_kernel(gate_hbm, up_hbm, down_hbm, *refs):
    gate_ref, up_ref, across_ref, down_ref, sems = refs[-5:]
    held = (gate_ref, up_ref, down_ref)
    loads = [
        pltpu.make_async_copy(src, dst, sems.at[i])
        for i, (src, dst) in enumerate(zip((gate_hbm, up_hbm, down_hbm), held))
    ]
    for load in loads:
        load.start()
    hidden = gate_ref.shape[0]
    for i, (load, ref) in enumerate(zip(loads, held)):
        load.wait()
        across_ref[:, i * hidden : (i + 1) * hidden] = ref[...].T


def expert_kernel(inputs, *refs):
    wg_ref, wu_ref, across_ref = refs[inputs : inputs + 3]
    zs, ms, (keep_ref, hid_ref, send_ref) = refs[:inputs], refs[inputs + 3 : -3], refs[-3:]
    features = wg_ref.shape[1]
    hidden = wg_ref.shape[0]
    fold = features // MAIN
    half = features // 2
    core = lax.axis_index("dp")
    pair = 2 * MAIN
    per = GROUP // SPLIT
    held = GROUP // len(zs)
    rows_in = held * pair
    groups = zs[0].shape[0] // rows_in

    def work(g):
        if groups == 1:
            src = slice(0, rows_in)
            all_rows = slice(0, (GROUP + 1) * pair)
        else:
            src = pl.ds(pl.multiple_of(g * rows_in, rows_in), rows_in)
            dst = pl.ds(pl.multiple_of(g * per * MAIN, per * MAIN), per * MAIN)
            all_rows = pl.ds(pl.multiple_of(g * (GROUP + 1) * pair, pair), (GROUP + 1) * pair)
        main = [z[src, :features] for z in zs]
        bent = jnp.concatenate([z[src, features : features + fold] for z in zs], axis=0)
        tiles = [z[src, features + fold :].astype(F32) for z in zs]
        n = GROUP * pair
        r, q = iota((n, n), 0), iota((n, n), 1)
        swap = ((r & 8) == (q & 8)) & ((r >> 4) == (q & 7)) & ((r & 7) == (q >> 4))
        flat = dot(swap.astype(BF16), bent, (1, 0)).astype(BF16)
        ninth = jnp.concatenate([flat[c * pair : (c + 1) * pair] for c in range(MAIN)], axis=1)
        rows = jnp.concatenate(main + [ninth], axis=0)
        pre = dot(rows, across_ref[...], (1, 0))
        pre_gate, pre_up, back = (pre[:, i * hidden : (i + 1) * hidden] for i in range(3))
        pieces = GROUP + 1
        upper = lambda v: v.reshape(pieces, 2, MAIN, hidden)[:, 0].reshape(pieces * MAIN, hidden)
        lower = lambda v: v.reshape(pieces, 2, MAIN, hidden)[:, 1].reshape(pieces * MAIN, hidden)
        pre_gate, pre_up, back = upper(pre_gate), upper(pre_up), lower(back)
        columns = []
        last = jnp.zeros((MAIN, 1), F32)
        seat = iota((MAIN, 1), 0)
        for p in range(GROUP):
            tile = tiles[p // held][(p % held) * pair : (p % held) * pair + MAIN]
            columns.append(tile[:, 0:1])
            last = jnp.where(seat == p, tile[:, 1:2], last)
        gate = jnp.concatenate(columns + [last], axis=0)
        sig = 1.0 / (1.0 + jnp.exp(-pre_gate))
        silu = pre_gate * sig
        slope = sig * (1.0 + pre_gate * (1.0 - sig))
        act = silu * pre_up
        combine = jnp.sum(back * act, axis=1, keepdims=True)
        scaled = gate * act
        gated = gate * back
        g_gate = (gated * slope * pre_up).astype(BF16)
        g_up = (gated * silu).astype(BF16)
        part = dot(g_gate, wg_ref[...], (1, 0)) + dot(g_up, wu_ref[...], (1, 0))
        tail = part[GROUP * MAIN :].astype(BF16).astype(F32)
        stack = jnp.concatenate([tail[:, c * fold : (c + 1) * fold] for c in range(MAIN)], axis=0)
        n = GROUP * MAIN
        r, q = iota((n, n), 0), iota((n, n), 1)
        turn = ((r >> 3) == (q & 7)) & ((r & 7) == (q >> 3))
        folded = dot(turn.astype(BF16), stack.astype(BF16), (1, 0))
        lane = iota((MAIN, TILE), 1)
        notes = []
        for p in range(GROUP):
            at = GROUP * MAIN + p
            notes.append(
                jnp.where(
                    lane == 0,
                    combine[p * MAIN : (p + 1) * MAIN],
                    jnp.where(lane == 1, combine[at : at + 1], 0.0),
                )
            )
        for i, m in enumerate(ms):
            if groups == 1:
                dst = slice(0, m.shape[0])
            at, size = (i, m.shape[0] // MAIN) if groups == 1 else (i * per, per)
            span = slice(at * MAIN, (at + size) * MAIN)
            m[dst, :features] = part[span].astype(BF16)
            m[dst, features : features + fold] = folded[span].astype(BF16)
            m[dst, features + fold :] = jnp.concatenate(notes[at : at + size], axis=0).astype(BF16)
        none = jnp.zeros((pieces, MAIN, hidden), F32)

        def lay(v, place):
            v = v.astype(F32).reshape(pieces, MAIN, hidden)
            both = [v, none] if place == 0 else [none, v]
            return jnp.stack(both, axis=1).reshape(pieces * 2 * MAIN, hidden).astype(BF16)

        hid = [lay(g_gate, 0), lay(g_up, 0), lay(scaled, 1)]
        low, high = rows[:, :half], rows[:, half:]
        keep_ref[all_rows, :] = jnp.where(core == 0, low, high)
        send_ref[all_rows, :half] = jnp.where(core == 0, high, low)
        for i, h in enumerate(hid):
            hid_ref[all_rows, i * hidden : (i + 1) * hidden] = h
            send_ref[all_rows, half + i * hidden : half + (i + 1) * hidden] = h

    if groups == 1:
        work(0)
    else:
        lax.fori_loop(0, groups, lambda g, c: (work(g), c)[1], 0)


def weights_kernel(keep_ref, hid_ref, peer_ref, gate_ref, up_ref, down_ref):
    half = keep_ref.shape[1]
    hidden = gate_ref.shape[0]
    outs = (gate_ref, up_ref, down_ref)
    for i, out in enumerate(outs):
        cols = slice(i * hidden, (i + 1) * hidden)
        far = slice(half + i * hidden, half + (i + 1) * hidden)
        total = dot(hid_ref[:, cols], keep_ref[...], (0, 0))
        total = total + dot(peer_ref[:, far], peer_ref[:, :half], (0, 0))
        out[...] = total.astype(BF16)


def finish_kernel(picks_ref, rank_ref, o0, o1, o2, o3, *rest):
    far, (grad_hbm, comb_hbm, grad_ref, comb_ref, sems) = rest[:-5], rest[-5:]
    window = 1 + len(far)
    quad = lax.axis_index("expert") // SPLIT
    picks = picks_ref[...]
    experts = [quad ^ k for k in range(window)]
    ranks = [rank_ref[k : k + 1, :] for k in range(window)]
    features = grad_ref.shape[1]
    fold = features // MAIN
    toks = picks.shape[1]
    seat = iota((MAIN, toks), 0).astype(F32)
    mains = [(r == seat).astype(F32) for r in ranks]
    lasts = [(r == float(MAIN)).astype(F32) for r in ranks]
    blocks = [(0, o[:MAIN, :].astype(F32)) for o in (o0, o1, o2, o3)]
    blocks += [(1 + k, f[...].astype(F32)) for k, f in enumerate(far)]
    terms = [jnp.zeros((1, toks), F32) for _ in range(window)]
    for k, v in blocks:
        note = v[:, features + fold :]
        terms[k] = terms[k] + jnp.sum(mains[k] * note[:, 0:1], axis=0, keepdims=True)
        terms[k] = terms[k] + lasts[k] * note[0:1, 1:2]
    comb = jnp.zeros(picks.shape, F32)
    for k in range(window):
        comb = comb + jnp.where(picks == experts[k], terms[k], 0.0)
    comb_ref[...] = comb
    stores = [pltpu.make_async_copy(comb_ref, comb_hbm, sems.at[PIECES])]
    stores[0].start()
    row = iota((MAIN, toks), 0)
    each = MAIN // PIECES
    for c in range(MAIN):
        cols = slice(c * fold, (c + 1) * fold)
        left, right = [], []
        for k, v in blocks:
            left += [mains[k], jnp.where(row == c, lasts[k], 0.0)]
            right += [v[:, cols], v[:, features : features + fold]]
        left = jnp.concatenate(left, axis=0).astype(BF16)
        right = jnp.concatenate(right, axis=0).astype(BF16)
        grad_ref[:, cols] = dot(left, right, (0, 0)).astype(BF16)
        if c % each == each - 1:
            done = slice((c + 1 - each) * fold, (c + 1) * fold)
            store = pltpu.make_async_copy(
                grad_ref.at[:, done], grad_hbm.at[:, done], sems.at[c // each]
            )
            store.start()
            stores.append(store)
    for store in stores:
        store.wait()


VM = pl.BlockSpec(memory_space=pltpu.VMEM)
HBM = pl.BlockSpec(memory_space=pltpu.HBM)
ANY = pl.BlockSpec(memory_space=pl.ANY)


def call(kernel, outs, name, args, flops, nbytes, room, specs=None, scratch=(), out_specs=None):
    specs = specs or [VM] * len(args)
    args = [
        pltpu.with_memory_space_constraint(a, pltpu.HBM) if s is HBM else a
        for a, s in zip(args, specs)
    ]
    return pl.pallas_call(
        kernel,
        out_shape=[jax.ShapeDtypeStruct(s, t) for s, t in outs],
        in_specs=specs,
        out_specs=out_specs or [VM] * len(outs),
        scratch_shapes=list(scratch),
        compiler_params=pltpu.CompilerParams(vmem_limit_bytes=min(VMEM_LIMIT, room * MIB)),
        cost_estimate=pl.CostEstimate(flops=flops, bytes_accessed=nbytes, transcendentals=0),
        name=name,
    )(*args)


def swap_by(block, mask):
    count = lax.axis_size("expert")
    return lax.ppermute(block, "expert", [(i, i ^ mask) for i in range(count)])


def body(tokens, out_grad, choices, gates, gate_weight, up_weight, down_weight):
    members = lax.axis_size("expert")
    toks, features = tokens.shape
    hidden = gate_weight.shape[2]
    window = members // SPLIT
    fold = features // MAIN
    half = features // 2
    width = features + fold + TILE
    picks, gates_t = choices.T, gates.T
    wg, wu, wd = gate_weight[0].T, up_weight[0].T, down_weight[0]
    groups = members // GROUP

    *packed, ranks = call(
        pack_kernel,
        [((2 * MAIN, width), BF16)] * window + [((-(-window // 8) * 8, toks), F32)],
        "pack",
        (picks, gates_t, tokens, out_grad),
        2 * (MAIN + 1) * window * toks * features * 2,
        4 * toks * features,
        6 + window,
        [HBM] * 4,
        [pltpu.VMEM(v.shape, v.dtype) for v in (picks, gates_t, tokens, out_grad)]
        + [pltpu.SemaphoreType.DMA((4,))],
    )
    own, others = packed[0], packed[1:]
    arrived = [swap_by(o, SPLIT * (k + 1)) for k, o in enumerate(others)]
    near = [own] + [swap_by(own, j) for j in range(1, SPLIT)]
    held = call(
        fetch_kernel,
        [(wg.shape, BF16), (wu.shape, BF16), ((features, 3 * hidden), BF16)],
        "fetch",
        (wg, wu, wd, near[1], near[2]),
        0,
        6 * features * hidden,
        12,
        [HBM] * 3 + [ANY] * 2,
        [pltpu.VMEM(wd.shape, BF16), pltpu.SemaphoreType.DMA((3,))],
    )
    from_far = arrived[0] if window == 2 else jnp.concatenate(arrived, axis=0)
    far = [from_far] + [swap_by(from_far, j) for j in range(1, SPLIT)]
    pairs = list(zip(near, far))
    if groups == 1:
        zs = [z for pair in pairs for z in pair]
    else:
        zs = [jnp.concatenate(pair, axis=0) for pair in pairs]

    all_rows = groups * (GROUP + 1) * 2 * MAIN
    kinds = [((MAIN, width), BF16)] * (GROUP - 2) + [((2 * MAIN, width), BF16)]
    if groups > 1:
        kinds = [((window * MAIN, width), BF16)] * SPLIT
    *messages, keep, hid, send = call(
        functools.partial(expert_kernel, len(zs)),
        kinds
        + [((all_rows, half), BF16), ((all_rows, 3 * hidden), BF16), ((all_rows, half + 3 * hidden), BF16)],
        "expert",
        (*zs, *held),
        2 * all_rows * features * hidden * 5,
        6 * features * hidden,
        10 + 6 * groups,
    )
    if groups == 1:
        home, away = messages[:-1:2], messages[1:-1:2]
    else:
        home, away = [m[:MAIN] for m in messages[:-1]], [m[MAIN:] for m in messages[:-1]]
    both = swap_by(messages[-1], SPLIT - 1)
    back = [away[0]] + [swap_by(away[j], j) for j in range(1, SPLIT - 1)] + [both]
    home = [home[0]] + [swap_by(home[j], j) for j in range(1, SPLIT - 1)]
    send, first = lax.optimization_barrier((send, back[2]))
    back[2] = first
    peer = lax.ppermute(send, "dp", [(0, 1), (1, 0)])
    peer, *rest = lax.optimization_barrier((peer, *home[:0:-1]))
    home = home[:1] + rest[::-1]
    gate_grad, up_grad, down_grad = call(
        weights_kernel,
        [((hidden, half), BF16)] * 3,
        "weights",
        (keep, hid, peer),
        2 * 2 * all_rows * half * hidden * 3,
        6 * half * hidden,
        6 + 2 * groups,
    )
    *parts, both = back
    total = sum([b.astype(F32) for b in parts[::-1]], both[MAIN:].astype(F32)).astype(BF16)
    homes = [
        swap_by(total[k * MAIN : (k + 1) * MAIN], SPLIT * (k + 1)) for k in range(window - 1)
    ]
    gate_grad, up_grad, down_grad, *homes = lax.optimization_barrier(
        (gate_grad, up_grad, down_grad, *homes)
    )
    in_grad, combine = call(
        finish_kernel,
        [((toks, features), BF16), ((choices.shape[1], toks), F32)],
        "finish",
        (picks, ranks, *home, both, *homes),
        2 * toks * features * 16 * (SPLIT + window),
        2 * toks * features,
        6 + window,
        scratch=[
            pltpu.VMEM((toks, features), BF16),
            pltpu.VMEM((choices.shape[1], toks), F32),
            pltpu.SemaphoreType.DMA((PIECES + 1,)),
        ],
        out_specs=[HBM, HBM],
    )
    return (
        in_grad,
        combine.T,
        gate_grad.T[None],
        up_grad.T[None],
        down_grad[None],
    )


def solution(mesh):
    return jax.shard_map(
        body,
        mesh=mesh,
        in_specs=(
            P(("groups", "expert", "dp"), None),
            P(("groups", "expert", "dp"), None),
            P(("groups", "expert", "dp"), None),
            P(("groups", "expert", "dp"), None),
            P("expert", None, None),
            P("expert", None, None),
            P("expert", None, None),
        ),
        out_specs=(
            P(("groups", "expert", "dp"), None),
            P(("groups", "expert", "dp"), None),
            P(("groups", "expert"), "dp", None),
            P(("groups", "expert"), "dp", None),
            P(("groups", "expert"), None, "dp"),
        ),
        check_vma=False,
    )
```
